256 devices in a mesh: rows: 32 (over y, x, core), feat: 8 (over z).
Axes of the slice: x: 4, y: 4, z: 8, core: 2. Of those that a mesh axis runs over, the one named last changes fastest.
Arguments:
- features: bfloat16 [65536, 768], P('rows', 'feat'), may hold values from -6 to 6
- pair_doc: int32 [768], P('rows'), may hold values from 0 to 127, as said below
- pair_label: int32 [768], P('rows'), may hold values from 0 to 127, as said below
- incidence: bfloat16 [768, 512, 512], P('rows'), may hold values from 0 to 1, as said below
- weight: bfloat16 [768, 768], P('feat'), may hold values from -0.21875 to 0.21875
- cotangent: bfloat16 [65536, 768], P('rows', 'feat'), may hold values from -6 to 6
Outputs:
- activated: bfloat16 [65536, 768], P('rows', 'feat')
- weight_grad: float32 [768, 768], P('feat')
- feature_grad: bfloat16 [65536, 768], P('rows', 'feat')
The draws below stay inside these ranges and needn't reach their ends.
Inputs may be any that keep to these rules, and one draw needn't show every extreme that they name: `pair_doc`: pair i belongs to rows index i // 24 and its document tile is one of that index's tiles, (i // 24) * 4 to (i // 24 + 1) * 4 - 1. `pair_label`: label block b is owned by rows index b // 4. The 24 pairs of one rows index go to exactly 8 distinct owners, 3 pairs to each. `incidence`: each entry is zero or a positive edge weight.
All inputs are finite; a program needn't handle non-finite values.
Results may differ from the reference program's by a relative error of at most 0.0066.
Values may be sent and summed in bfloat16 or wider, within the bound.
A program may use at most 128 MiB of HBM per device.

```python
import jax
import jax.numpy as jnp
from jax import lax

D = 768
TILE = 512
DT_DEV = 4
LB_DEV = 4
PAIRS_DEV = 24
CAPO = 3
NDT = 128
NDOC = 65536
NBLOCKS = 128
NLAB = 65536
NPAIRS = 768
N_ROWS = 32


def draw_pair_doc(key, part):
    key = jax.random.fold_in(key, 12)
    local_tiles = jax.random.randint(key, (N_ROWS, PAIRS_DEV), 0, DT_DEV)
    offsets = jnp.arange(N_ROWS, dtype=jnp.int32)[:, None] * DT_DEV
    return (local_tiles + offsets).reshape(-1).astype(jnp.int32)


def draw_pair_label(key, part):
    key = jax.random.fold_in(key, 11)
    hot_key, pick_key, block_key = jax.random.split(key, 3)
    ranking = jax.random.permutation(hot_key, N_ROWS)
    popular = (ranking < max(1, N_ROWS // 8)).astype(jnp.int32)
    senders = jnp.arange(N_ROWS, dtype=jnp.int32)[:, None]
    targets = jnp.arange(N_ROWS, dtype=jnp.int32)[None, :]
    following = (targets == (senders + 1) % N_ROWS).astype(jnp.int32)
    preceding = (targets == (senders + N_ROWS - 1) % N_ROWS).astype(jnp.int32)
    opposite = (targets == (senders + N_ROWS // 2) % N_ROWS).astype(jnp.int32)
    scores = jax.random.randint(pick_key, (N_ROWS, N_ROWS), 0, 1000) + 1000 * popular[None, :]
    scores = scores + 3000 * preceding + 2900 * following + 2500 * opposite
    scores = scores * N_ROWS + targets
    chosen = jnp.argsort(-scores, axis=1)[:, :PAIRS_DEV // CAPO]
    owners = jnp.repeat(chosen, CAPO, axis=1)
    blocks = jax.random.randint(block_key, (N_ROWS, PAIRS_DEV), 0, LB_DEV)
    return (owners * LB_DEV + blocks).reshape(-1).astype(jnp.int32)


def draw_incidence(key, part):
    key = jax.random.fold_in(key, 13)
    mask_key, value_key = jax.random.split(key)
    pattern = jax.random.bernoulli(mask_key, 0.4, (NPAIRS, TILE, TILE)).astype(jnp.float32)
    values = jax.random.uniform(value_key, (NPAIRS, TILE, TILE), jnp.float32, 0.1, 1.0)
    return (pattern * values).astype(jnp.bfloat16)


def levels(own_key, shape, shards, least, top_value):
    gain, own = 1.0, jax.random.fold_in(own_key, 6)
    for dim, shards_of in shards:
        steps = jnp.exp(jax.random.uniform(jax.random.fold_in(own, dim), (shards_of,), jnp.float32, least / len(shards), top_value / len(shards)))
        gain = gain * jnp.repeat(steps, shape[dim] // shards_of).reshape([-1 if axis == dim else 1 for axis in range(len(shape))])
    return gain


def scatter_about(key, dims, scale, bound, cuts=(), kind=jnp.bfloat16):
    result = jax.random.normal(key, dims, jnp.float32) * scale
    if len(cuts) > 0:
        result = levels(key, dims, cuts, -0.22, 0.18) * result
    return jnp.clip(result, min=-bound, max=bound).astype(kind)


def setup_inputs(seed: int = 0) -> dict:
    arg_keys = jax.random.split(jax.random.key(seed), 7)
    features = scatter_about(arg_keys[0], (NDOC, D), 1.0, 6.0, ((0, 32), (1, 8)))
    pair_doc = draw_pair_doc(jax.random.fold_in(arg_keys[6], 71), 0)
    pair_label = draw_pair_label(jax.random.fold_in(arg_keys[6], 71), 0)
    incidence = draw_incidence(jax.random.fold_in(arg_keys[6], 71), 0)
    weight = scatter_about(arg_keys[4], (D, D), D ** -0.5, 0.21875, ((0, 8),))
    cotangent = scatter_about(arg_keys[5], (NLAB, D), 1.0, 6.0, ((0, 32), (1, 8)))
    return dict(features=features, pair_doc=pair_doc, pair_label=pair_label, incidence=incidence, weight=weight, cotangent=cotangent)


message_scale = 0.0625


def reference(features, pair_doc, pair_label, incidence, weight, cotangent):
    doc_stack = features.reshape(NDT, TILE, D)

    def forward_step(totals, index):
        piece = doc_stack[pair_doc[index]]
        product = jnp.dot(incidence[index].T, piece, preferred_element_type=jnp.float32)
        rounded = (message_scale * product).astype(jnp.bfloat16)
        rounded = lax.optimization_barrier(rounded)
        return totals.at[pair_label[index]].add(rounded.astype(jnp.float32)), None

    totals, _ = lax.scan(forward_step, jnp.zeros((NBLOCKS, TILE, D), jnp.float32),
                         jnp.arange(NPAIRS, dtype=jnp.int32))
    messages = totals.reshape(NLAB, D).astype(jnp.bfloat16)
    mixed = jnp.dot(messages, weight, preferred_element_type=jnp.float32)
    gate_value = jax.nn.sigmoid(mixed)
    activated = (mixed * gate_value).astype(jnp.bfloat16)
    slope = gate_value * (1.0 + mixed * (1.0 - gate_value))
    grad_mixed = (cotangent.astype(jnp.float32) * slope).astype(jnp.bfloat16)
    weight_grad = jnp.dot(messages.T, grad_mixed, preferred_element_type=jnp.float32)
    grad_messages = jnp.dot(grad_mixed, weight.T, preferred_element_type=jnp.float32).astype(jnp.bfloat16)
    grad_blocks = grad_messages.reshape(NBLOCKS, TILE, D)

    def backward_step(totals_doc, index):
        term = jnp.dot(incidence[index], grad_blocks[pair_label[index]], preferred_element_type=jnp.float32)
        return totals_doc.at[pair_doc[index]].add(term), None

    doc_totals, _ = lax.scan(backward_step, jnp.zeros((NDT, TILE, D), jnp.float32),
                             jnp.arange(NPAIRS, dtype=jnp.int32))
    feature_grad = doc_totals.reshape(NDOC, D).astype(jnp.bfloat16)
    return activated, weight_grad, feature_grad
```

```python
import functools

import jax
import jax.numpy as jnp
from jax import lax
from jax.experimental import pallas as pl
from jax.experimental.pallas import tpu as pltpu
from jax.sharding import PartitionSpec as P

MESH = pl.DeviceIdType.MESH
message_scale = 0.0625

SIDE = 4
FEAT = 8
LB = 4
CAP = 3
TILE = 512
PAIRS = 24
W = 96
D = 768
GROUP = 4
BLOCKS = 128
CHUNK = 256
VMEM_LIMIT = 60 * 1024 * 1024

f32, bf16 = jnp.float32, jnp.bfloat16


def forward_kernel(doc_ref, label_ref, feat_ref, inc_ref, msg_ref, table_ref):
    step = pl.program_id(0)
    rows = lax.axis_index("rows")

    @pl.when(step == 0)
    def _():
        msg_ref[PAIRS] = jnp.zeros((W, TILE), bf16)

        def clear(i, carry):
            table_ref[i] = PAIRS
            return carry

        lax.fori_loop(0, BLOCKS * CAP, clear, 0)

        def place(p, carry):
            base = label_ref[p] * CAP
            first = table_ref[base] == PAIRS
            second = table_ref[base + 1] == PAIRS
            spot = jnp.where(first, 0, jnp.where(second, 1, 2))
            table_ref[base + spot] = p
            return carry

        lax.fori_loop(0, PAIRS, place, 0)

    for k in range(GROUP):
        p = step * GROUP + k
        tile = doc_ref[p] - rows * (feat_ref.shape[1] // TILE)
        piece = feat_ref[:, pl.ds(pl.multiple_of(tile * TILE, TILE), TILE)]
        product = jnp.dot(piece, inc_ref[k], preferred_element_type=f32)
        msg_ref[p] = (message_scale * product).astype(bf16)


def forward_pairs(doc, label, feat, inc):
    return pl.pallas_call(
        forward_kernel,
        grid_spec=pltpu.PrefetchScalarGridSpec(
            num_scalar_prefetch=2,
            grid=(PAIRS // GROUP,),
            in_specs=[
                pl.BlockSpec((W, feat.shape[1]), lambda i, d, l: (0, 0)),
                pl.BlockSpec((GROUP, TILE, TILE), lambda i, d, l: (i, 0, 0)),
            ],
            out_specs=[
                pl.BlockSpec((PAIRS + 1, W, TILE), lambda i, d, l: (0, 0, 0)),
                pl.BlockSpec(memory_space=pltpu.SMEM),
            ],
        ),
        out_shape=[
            jax.ShapeDtypeStruct((PAIRS + 1, W, TILE), bf16),
            jax.ShapeDtypeStruct((BLOCKS * CAP,), jnp.int32),
        ],
        compiler_params=pltpu.CompilerParams(vmem_limit_bytes=VMEM_LIMIT),
    )(doc, label, feat, inc)


def backward_kernel(doc_ref, label_ref, *refs):
    grads, inc_ref, out_ref, acc = refs[:GROUP], refs[GROUP], refs[GROUP + 1], refs[GROUP + 2]
    step = pl.program_id(0)
    rows = lax.axis_index("rows")
    tiles = acc.shape[0]

    @pl.when(step == 0)
    def _():
        acc[...] = jnp.zeros_like(acc)

    for k in range(GROUP):
        tile = doc_ref[step * GROUP + k] - rows * tiles
        acc[tile] += lax.dot_general(
            grads[k][0], inc_ref[k], (((1,), (1,)), ((), ())), preferred_element_type=f32
        )

    @pl.when(step == PAIRS // GROUP - 1)
    def _():
        for t in range(tiles):
            out_ref[:, t * TILE : (t + 1) * TILE] = acc[t].astype(bf16)


def backward_pairs(doc, label, grads, inc, width):
    def pick(k):
        return lambda i, d, l: (l[i * GROUP + k], 0, 0)

    return pl.pallas_call(
        backward_kernel,
        grid_spec=pltpu.PrefetchScalarGridSpec(
            num_scalar_prefetch=2,
            grid=(PAIRS // GROUP,),
            in_specs=[pl.BlockSpec((1, W, TILE), pick(k)) for k in range(GROUP)]
            + [pl.BlockSpec((GROUP, TILE, TILE), lambda i, d, l: (i, 0, 0))],
            out_specs=pl.BlockSpec((W, width), lambda i, d, l: (0, 0)),
            scratch_shapes=[pltpu.VMEM((width // TILE, W, TILE), f32)],
        ),
        out_shape=jax.ShapeDtypeStruct((W, width), bf16),
        compiler_params=pltpu.CompilerParams(vmem_limit_bytes=VMEM_LIMIT),
    )(doc, label, *([grads] * GROUP), inc)


def wait(ref, sem):
    pltpu.make_async_copy(ref, ref, sem).wait()


def offset(i):
    return 2 - i + 3 * (i // 2) - 2 * (i // 3)


def exchange_kernel(
    table, msg, weight, cot,
    act_out, wg_out, grads,
    sib_send, sib_recv, s1_send, s1_recv, s2_send, s2_recv, t1_send, t1_recv, t2_send, t2_recv,
    summed, xin, wfull, cot_in, act_buf, gm_buf, gmt_buf,
    wgp, wgc_recv, wgz_send, wgz_recv, wx_send, wx_recv, wy_send, wy_recv, wf_send, wf_recv, wg_half,
    sib_ss, sib_rs, s1_ss, s1_rs, s2_ss, s2_rs, t_ss, t1_rs, t2_rs,
    z_ss, x_rs, w_rs, cot_rs, act_rs, gz_rs, local_sem,
    ag_ss, p1_rs, p2_rs, q1_rs, q2_rs, pair_rs,
    wg_ss, wgc_rs, wgz_rs, wx_rs, wy_rs, wf_rs, wl_rs,
):
    r, z = lax.axis_index("rows"), lax.axis_index("feat")
    core, x, y = lax.rem(r, 2), lax.rem(r // 2, SIDE), r // (2 * SIDE)

    def around(value, step):
        return lax.rem(value + step + 2 * SIDE, SIDE)

    def row_of(yy, xx, cc):
        return (yy * SIDE + xx) * 2 + cc

    place = ((x, y), (y, x))

    def owner(h, u, v, cc):
        return row_of(v, u, cc) if h == 0 else row_of(u, v, cc)

    def near(h, du, dv):
        u, v = place[h]
        return {"rows": owner(h, around(u, du), around(v, dv), core), "feat": z}

    sibling = {"rows": row_of(y, x, 1 - core), "feat": z}

    def along_z(d):
        return lax.rem(z + d, FEAT)

    def send(src, dst, ss, rs, target):
        pltpu.make_async_remote_copy(
            src_ref=src, dst_ref=dst, send_sem=ss, recv_sem=rs, device_id=target, device_id_type=MESH
        ).start()

    barrier = pltpu.get_barrier_semaphore()
    partners = [sibling]
    for d in range(1, SIDE):
        partners += [near(0, d, 0), near(1, d, 0)]
    for d in range(1, FEAT):
        partners.append({"rows": r, "feat": along_z(d)})
    for target in partners:
        pl.semaphore_signal(barrier, inc=1, device_id=target, device_id_type=MESH)
    pl.semaphore_wait(barrier, len(partners))

    def block_id(h, u, v, j, cc):
        return owner(h, u, v, cc) * LB + 2 * h + j

    def own_part(block):
        base = block * CAP
        total = msg[table[base]].astype(f32)
        for k in range(1, CAP):
            total = total + msg[table[base + k]].astype(f32)
        return total

    def slot(g, i, h, j):
        return ((g * SIDE + i) * 2 + h) * 2 + j

    def pair_part(g, du, i):
        for h in range(2):
            u, v = place[h]
            for j in range(2):
                k = slot(g, i, h, j)
                block = block_id(h, around(u, du), around(v, offset(i)), j, 1 - core)
                sib_send[k] = own_part(block).astype(bf16)
                send(sib_send.at[k], sib_recv.at[k], sib_ss, sib_rs.at[k], sibling)

    def merged(g, du, i, h, j):
        u, v = place[h]
        k = slot(g, i, h, j)
        part = own_part(block_id(h, around(u, du), around(v, offset(i)), j, core))
        wait(sib_recv.at[k], sib_rs.at[k])
        return part + sib_recv[k].astype(f32)

    def loop(n, body):
        lax.fori_loop(0, n, lambda i, c: (body(i), c)[1], 0)

    loop(SIDE, lambda i: pair_part(0, 2, i))

    def first(i):
        for h in range(2):
            for j in range(2):
                k = slot(0, i, h, j)
                s1_send[k] = merged(0, 2, i, h, j).astype(bf16)
                send(s1_send.at[k], s1_recv.at[k], s1_ss, s1_rs.at[k], near(h, 1 - 2 * j, 0))
        pair_part(1, 1, i)
        pair_part(2, -1, i)

    loop(SIDE, first)

    def spread(d):
        zz = along_z(d)
        target = {"rows": r, "feat": zz}
        mine = pl.ds(pl.multiple_of(z * W, W), W)
        send(weight, wfull.at[mine, :], z_ss.at[0], w_rs.at[z], target)
        lanes = pl.ds(pl.multiple_of(zz * CHUNK, CHUNK), CHUNK)
        send(cot.at[:, lanes], cot_in.at[mine, :], z_ss.at[1], cot_rs.at[z], target)

    lax.fori_loop(1, FEAT, lambda d, c: (spread(d), c)[1], 0)
    own_rows = pl.ds(pl.multiple_of(z * W, W), W)
    own_lanes = pl.ds(pl.multiple_of(z * CHUNK, CHUNK), CHUNK)
    wfull[own_rows, :] = weight[...]
    cot_in[own_rows, :] = cot[:, own_lanes]

    def second(i):
        for h in range(2):
            for way in range(2):
                du = 1 - 2 * way
                for j in (1 - way, way):
                    k = slot(way, i, h, j)
                    total = merged(1 + way, du, i, h, j)
                    if j == way:
                        q = slot(0, i, h, j)
                        wait(s1_recv.at[q], s1_rs.at[q])
                        total = total + s1_recv[q].astype(f32)
                    s2_send[k] = total.astype(bf16)
                    send(s2_send.at[k], s2_recv.at[k], s2_ss, s2_rs.at[k], near(h, du, 0))
        pair_part(3, 0, i)

    loop(SIDE, second)

    def column(i, h, j):
        total = merged(3, 0, i, h, j)
        for way in range(2):
            k = slot(way, i, h, j)
            wait(s2_recv.at[k], s2_rs.at[k])
            total = total + s2_recv[k].astype(f32)
        return total

    for h in range(2):
        for j in range(2):
            k = 2 * h + j
            t1_send[k] = column(0, h, j).astype(bf16)
            send(t1_send.at[k], t1_recv.at[k], t_ss.at[0], t1_rs.at[k], near(h, 0, 1 - 2 * j))
    for way in range(2):
        for h in range(2):
            for j in (1 - way, way):
                k = (way * 2 + h) * 2 + j
                total = column(1 + way, h, j)
                if j == way:
                    q = 2 * h + j
                    wait(t1_recv.at[q], t1_rs.at[q])
                    total = total + t1_recv[q].astype(f32)
                t2_send[k] = total.astype(bf16)
                send(t2_send.at[k], t2_recv.at[k], t_ss.at[1], t2_rs.at[k], near(h, 0, 1 - 2 * way))
    for h in range(2):
        for j in range(2):
            total = column(3, h, j)
            for way in range(2):
                k = (way * 2 + h) * 2 + j
                wait(t2_recv.at[k], t2_rs.at[k])
                total = total + t2_recv[k].astype(f32)
            summed[2 * h + j] = total.astype(bf16)

    def half_lanes(zz):
        return pl.ds(pl.multiple_of(lax.rem(zz, 2) * CHUNK, CHUNK), CHUNK)

    def gather_features(d):
        zz = along_z(d)
        send(summed.at[zz // 2, :, half_lanes(zz)], xin.at[own_rows, :], z_ss.at[2], x_rs.at[z],
             {"rows": r, "feat": zz})

    lax.fori_loop(1, FEAT, lambda d, c: (gather_features(d), c)[1], 0)
    xin[own_rows, :] = summed[z // 2, :, half_lanes(z)]

    def arrive(ref, sems):
        def one(d):
            zz = along_z(d)
            wait(ref.at[pl.ds(pl.multiple_of(zz * W, W), W), :], sems.at[zz])

        lax.fori_loop(1, FEAT, lambda d, c: (one(d), c)[1], 0)

    arrive(wfull, w_rs)
    arrive(cot_in, cot_rs)
    arrive(xin, x_rs)

    def mix(o):
        rows = pl.ds(pl.multiple_of(o * CHUNK, CHUNK), CHUNK)
        mixed = lax.dot_general(
            wfull[:, rows], xin[...], (((0,), (0,)), ((), ())), preferred_element_type=f32
        )
        gate = jax.nn.sigmoid(mixed)
        act_buf[rows, :] = (mixed * gate).astype(bf16)
        slope = gate * (1.0 + mixed * (1.0 - gate))
        gm_buf[rows, :] = (cot_in[rows, :].astype(f32) * slope).astype(bf16)

    loop(D // CHUNK, mix)

    def unmix(o):
        rows = pl.ds(pl.multiple_of(o * CHUNK, CHUNK), CHUNK)
        gmt_buf[rows, :] = jnp.dot(wfull[rows, :], gm_buf[...], preferred_element_type=f32).astype(bf16)

    loop(D // CHUNK, unmix)

    def give_back(d):
        zz = along_z(d)
        rows = pl.ds(pl.multiple_of(zz * W, W), W)
        target = {"rows": r, "feat": zz}
        send(gmt_buf.at[rows, :], grads.at[r * LB + z // 2, :, half_lanes(z)], z_ss.at[3], gz_rs.at[z], target)

    def give_act(d):
        zz = along_z(d)
        rows = pl.ds(pl.multiple_of(zz * W, W), W)
        target = {"rows": r, "feat": zz}
        send(act_buf.at[rows, :], act_out.at[:, own_lanes], z_ss.at[4], act_rs.at[z], target)

    lax.fori_loop(1, FEAT, lambda d, c: (give_back(d), c)[1], 0)
    own_grad = pltpu.make_async_copy(
        gmt_buf.at[own_rows, :], grads.at[r * LB + z // 2, :, half_lanes(z)], local_sem.at[0]
    )
    own_grad.start()
    lax.fori_loop(1, FEAT, lambda d, c: (give_act(d), c)[1], 0)
    own_act = pltpu.make_async_copy(act_buf.at[own_rows, :], act_out.at[:, own_lanes], local_sem.at[1])
    own_act.start()

    HALF = W // 2

    def weight_term(s):
        rows = pl.ds(pl.multiple_of(s * CHUNK, CHUNK), CHUNK)
        wgp[rows, :] = lax.dot_general(
            xin[rows, :], gm_buf[...], (((1,), (1,)), ((), ())), preferred_element_type=f32
        )

    loop(D // CHUNK, weight_term)

    def slab(s, cc):
        return pl.ds(pl.multiple_of(s * W + cc * HALF, HALF), HALF)

    def to_sibling(s):
        send(wgp.at[slab(s, 1 - core), :], wgc_recv.at[s], wg_ss.at[0], wgc_rs.at[s], sibling)

    loop(FEAT, to_sibling)

    def to_z(d):
        zz = along_z(d)
        wait(wgc_recv.at[zz], wgc_rs.at[zz])
        wgz_send[zz] = (wgp[slab(zz, core), :] + wgc_recv[zz]).astype(bf16)
        send(wgz_send.at[zz], wgz_recv.at[z], wg_ss.at[1], wgz_rs.at[z], {"rows": r, "feat": zz})

    lax.fori_loop(1, FEAT, lambda d, c: (to_z(d), c)[1], 0)
    wait(wgc_recv.at[z], wgc_rs.at[z])

    own_grad.wait()

    def grads_in(d):
        zz = along_z(d)
        wait(grads.at[r * LB + zz // 2, :, half_lanes(zz)], gz_rs.at[zz])

    lax.fori_loop(1, FEAT, lambda d, c: (grads_in(d), c)[1], 0)

    def share(block):
        send(grads.at[block], grads.at[block], ag_ss, pair_rs, sibling)

    def pass_on(block, rs, target):
        send(grads.at[block], grads.at[block], ag_ss, rs, target)

    def at(h, du, dv, j):
        u, v = place[h]
        return block_id(h, around(u, du), around(v, dv), j, core)

    def four(way, h, j):
        return (way * 2 + h) * 2 + j

    for way in range(2):
        for h in range(2):
            for j in (way, 1 - way):
                pass_on(at(h, 0, 0, j), p1_rs.at[four(way, h, j)], near(h, 1 - 2 * way, 0))
    for h in range(2):
        for j in range(2):
            share(at(h, 0, 0, j))

    def second_axis(g, du, h, j):
        for way in range(2):
            pass_on(at(h, du, 0, j), q1_rs.at[g * 8 + four(way, h, j)], near(h, 0, 1 - 2 * way))

    for h in range(2):
        for j in range(2):
            second_axis(0, 0, h, j)
    for way in range(2):
        du = 2 * way - 1
        for h in range(2):
            for j in (way, 1 - way):
                block = at(h, du, 0, j)
                wait(grads.at[block], p1_rs.at[four(way, h, j)])
                if j == way:
                    pass_on(block, p2_rs.at[2 * h + way], near(h, 1 - 2 * way, 0))
                second_axis(1 + way, du, h, j)
                share(block)
    for h in range(2):
        for j in range(2):
            block = at(h, 2, 0, j)
            wait(grads.at[block], p2_rs.at[2 * h + j])
            second_axis(3, 2, h, j)
            share(block)

    acc = wgp[slab(z, core), :] + wgc_recv[z]
    for d in range(1, FEAT):
        zz = along_z(d)
        wait(wgz_recv.at[zz], wgz_rs.at[zz])
        acc = acc + wgz_recv[zz].astype(f32)
    tiles = [acc[8 * a : 8 * a + 8, 128 * b : 128 * b + 128] for a in range(6) for b in range(6)]
    for t in range(36):
        wx_send[t // 9, t % 9] = tiles[t]
    for d in range(1, SIDE):
        xx = around(x, d)
        send(wx_send.at[xx], wx_recv.at[x], wg_ss.at[2], wx_rs.at[x], near(0, d, 0))

    offs = (0, -1, 1, 2)

    def take(g):
        du = offs[g]
        for way in range(2):
            dv = 2 * way - 1
            for h in range(2):
                for j in (way, 1 - way):
                    block = at(h, du, dv, j)
                    wait(grads.at[block], q1_rs.at[g * 8 + four(way, h, j)])
                    if j == way:
                        pass_on(block, q2_rs.at[g * 4 + 2 * h + way], near(h, 0, 1 - 2 * way))
                    share(block)

    take(0)
    total = wx_send[x]
    for d in range(1, SIDE):
        xx = around(x, d)
        wait(wx_recv.at[xx], wx_rs.at[xx])
        total = total + wx_recv[xx]
    wy_send[...] = total
    wy_recv[y] = total
    for d in range(1, SIDE):
        send(wy_send, wy_recv.at[y], wg_ss.at[3], wy_rs.at[y], near(1, d, 0))
    take(1)
    for d in range(1, SIDE):
        yy = around(y, d)
        wait(wy_recv.at[yy], wy_rs.at[yy])
    total = (wy_recv[0] + wy_recv[1]) + (wy_recv[2] + wy_recv[3])
    wf_send[...] = total
    wf_recv[x] = total
    for d in range(1, SIDE):
        send(wf_send, wf_recv.at[x], wg_ss.at[4], wf_rs.at[x], near(0, d, 0))
    take(2)
    for d in range(1, SIDE):
        xx = around(x, d)
        wait(wf_recv.at[xx], wf_rs.at[xx])
    for t in range(36):
        a, b = t // 6, t % 6
        wg_half[8 * a : 8 * a + 8, 128 * b : 128 * b + 128] = wf_recv[t // 9, t % 9]
    mine = pl.ds(pl.multiple_of(core * HALF, HALF), HALF)
    other = pl.ds(pl.multiple_of((1 - core) * HALF, HALF), HALF)
    send(wg_half, wg_out.at[mine, :], wg_ss.at[5], wl_rs, sibling)
    own_wg = pltpu.make_async_copy(wg_half, wg_out.at[mine, :], local_sem.at[2])
    own_wg.start()
    take(3)
    for g in range(4):
        for h in range(2):
            for j in range(2):
                block = at(h, offs[g], 2, j)
                wait(grads.at[block], q2_rs.at[g * 4 + 2 * h + j])
                share(block)

    own_wg.wait()
    wait(wg_out.at[other, :], wl_rs)
    own_act.wait()

    def act_in(d):
        zz = along_z(d)
        wait(act_out.at[:, pl.ds(pl.multiple_of(zz * CHUNK, CHUNK), CHUNK)], act_rs.at[zz])

    lax.fori_loop(1, FEAT, lambda d, c: (act_in(d), c)[1], 0)
    wait(grads.at[pl.ds(0, 64)], pair_rs)
    wait(grads.at[pl.ds(0, 124)], ag_ss)
    wait(sib_send, sib_ss)
    wait(s1_send, s1_ss)
    wait(s2_send, s2_ss)
    wait(t1_send, t_ss.at[0])
    wait(t2_send, t_ss.at[1])
    seven = pl.ds(0, (FEAT - 1) * W)
    wait(wfull.at[seven, :], z_ss.at[0])
    for k in range(1, 5):
        wait(cot_in.at[seven, :], z_ss.at[k])
    wait(wgc_recv, wg_ss.at[0])
    wait(wgz_send.at[pl.ds(0, FEAT - 1)], wg_ss.at[1])
    for k in (2, 3, 4):
        wait(wx_send.at[pl.ds(0, SIDE - 1)], wg_ss.at[k])
    wait(wg_half, wg_ss.at[5])


def exchange(table, msg, weight, cot):
    dma = pltpu.SemaphoreType.DMA
    block = (W, TILE)
    vmem = pltpu.VMEM
    any_spec = pl.BlockSpec(memory_space=pl.ANY)
    vmem_spec = pl.BlockSpec(memory_space=pltpu.VMEM)
    return pl.pallas_call(
        exchange_kernel,
        in_specs=[pl.BlockSpec(memory_space=pltpu.SMEM), vmem_spec, vmem_spec, vmem_spec],
        out_specs=[any_spec] * 3,
        out_shape=[
            jax.ShapeDtypeStruct(cot.shape, bf16),
            jax.ShapeDtypeStruct((W, D), f32),
            jax.ShapeDtypeStruct((BLOCKS, *block), bf16),
        ],
        scratch_shapes=[
            vmem((64, *block), bf16), vmem((64, *block), bf16),
            vmem((16, *block), bf16), vmem((16, *block), bf16),
            vmem((32, *block), bf16), vmem((32, *block), bf16),
            vmem((4, *block), bf16), vmem((4, *block), bf16),
            vmem((8, *block), bf16), vmem((8, *block), bf16),
            vmem((LB, *block), bf16),
            vmem((D, CHUNK), bf16), vmem((D, D), bf16), vmem((D, CHUNK), bf16),
            vmem((D, CHUNK), bf16), vmem((D, CHUNK), bf16), vmem((D, CHUNK), bf16),
            vmem((D, D), f32), vmem((FEAT, W // 2, D), f32),
            vmem((FEAT, W // 2, D), bf16), vmem((FEAT, W // 2, D), bf16),
            vmem((SIDE, 9, 8, 128), f32), vmem((SIDE, 9, 8, 128), f32),
            vmem((9, 8, 128), f32), vmem((SIDE, 9, 8, 128), f32),
            vmem((9, 8, 128), f32), vmem((SIDE, 9, 8, 128), f32),
            vmem((W // 2, D), f32),
            dma, dma((64,)), dma, dma((16,)), dma, dma((32,)), dma((2,)), dma((4,)), dma((8,)),
            dma((5,)), dma((FEAT,)), dma((FEAT,)), dma((FEAT,)), dma((FEAT,)), dma((FEAT,)), dma((3,)),
            dma, dma((8,)), dma((4,)), dma((32,)), dma((16,)), dma,
            dma((6,)), dma((FEAT,)), dma((FEAT,)), dma((SIDE,)), dma((SIDE,)), dma((SIDE,)), dma,
        ],
        compiler_params=pltpu.CompilerParams(
            collective_id=0, has_side_effects=True, vmem_limit_bytes=VMEM_LIMIT
        ),
    )(table, msg, weight, cot)


def local(features, pair_doc, pair_label, incidence, weight, cotangent):
    msg, table = forward_pairs(pair_doc, pair_label, features.T, incidence)
    act, weight_grad, grads = exchange(table, msg, weight, cotangent.T)
    feature_grad = backward_pairs(pair_doc, pair_label, grads, incidence, features.shape[0])
    return act.T, weight_grad, feature_grad.T


def solution(mesh):
    return jax.shard_map(
        local,
        mesh=mesh,
        in_specs=(
            P("rows", "feat"),
            P("rows"),
            P("rows"),
            P("rows", None, None),
            P("feat", None),
            P("rows", "feat"),
        ),
        out_specs=(P("rows", "feat"), P("feat", None), P("rows", "feat")),
        check_vma=False,
    )
```

```python
import functools

import jax
import jax.numpy as jnp
from jax import lax
from jax.experimental import pallas as pl
from jax.experimental.pallas import tpu as pltpu
from jax.sharding import PartitionSpec as P

MESH = pl.DeviceIdType.MESH
message_scale = 0.0625

SIDE = 4
FEAT = 8
LB = 4
CAP = 3
TILE = 512
PAIRS = 24
W = 96
D = 768
GROUP = 4
BLOCKS = 128
CHUNK = 256
PART = 128
BATCHES = PAIRS // GROUP
NONE = 2 * PAIRS
VMEM_LIMIT = 60 * 1024 * 1024

f32, bf16 = jnp.float32, jnp.bfloat16


def backward_kernel(doc_ref, label_ref, *refs):
    grads, inc_ref, out_ref, acc = refs[:GROUP], refs[GROUP], refs[GROUP + 1], refs[GROUP + 2]
    step = pl.program_id(0)
    rows = lax.axis_index("rows")
    tiles = acc.shape[0]

    @pl.when(step == 0)
    def _():
        acc[...] = jnp.zeros_like(acc)

    for k in range(GROUP):
        tile = doc_ref[step * GROUP + k] - rows * tiles
        grad = jnp.concatenate([grads[k][0, 0], grads[k][1, 0]], axis=1)
        acc[tile] += lax.dot_general(
            grad, inc_ref[k], (((1,), (1,)), ((), ())), preferred_element_type=f32
        )

    @pl.when(step == PAIRS // GROUP - 1)
    def _():
        for t in range(tiles):
            out_ref[:, t * TILE : (t + 1) * TILE] = acc[t].astype(bf16)


def backward_pairs(doc, label, grads, inc, width):
    def pick(k):
        return lambda i, d, l: (0, l[i * GROUP + k], 0, 0)

    return pl.pallas_call(
        backward_kernel,
        grid_spec=pltpu.PrefetchScalarGridSpec(
            num_scalar_prefetch=2,
            grid=(PAIRS // GROUP,),
            in_specs=[pl.BlockSpec((2, 1, W, CHUNK), pick(k)) for k in range(GROUP)]
            + [pl.BlockSpec((GROUP, TILE, TILE), lambda i, d, l: (i, 0, 0))],
            out_specs=pl.BlockSpec((W, width), lambda i, d, l: (0, 0)),
            scratch_shapes=[pltpu.VMEM((width // TILE, W, TILE), f32)],
        ),
        out_shape=jax.ShapeDtypeStruct((W, width), bf16),
        compiler_params=pltpu.CompilerParams(vmem_limit_bytes=VMEM_LIMIT),
    )(doc, label, *([grads] * GROUP), inc)


def wait(ref, sem):
    pltpu.make_async_copy(ref, ref, sem).wait()


def offset(i):
    return 2 - i + 3 * (i // 2) - 2 * (i // 3)


def exchange_kernel(
    doc_ref, label_ref, feat, inc, weight, cot,
    act_out, wg_out, grads,
    tiles, inc_buf, msg_a, msg_b, tab, tab_out, tab_in, tab_own, tab_sib,
    s1_send, s1_recv, s2_send, s2_recv, t1_send, t1_recv, t2_send, t2_recv,
    summed, xin, wfull, cot_in, act_buf, gm_buf, gmt_buf,
    wgp, wgc_recv, wgz_send, wgz_recv, wx_send, wx_recv, wy_send, wy_recv, wf_send, wf_recv, wg_half,
    inc_sem, tab_sems, sib_ss, sib_rs, s1_ss, s1_rs, s2_ss, s2_rs, t_ss, t1_rs, t2_rs,
    z_ss, x_rs, w_rs, cot_rs, act_rs, gz_rs, local_sem,
    ag_ss, p1_rs, p2_rs, q1_rs, q2_rs, pair_rs,
    wg_ss, wgc_rs, wgz_rs, wx_rs, wy_rs, wf_rs, wl_rs,
):
    r, z = lax.axis_index("rows"), lax.axis_index("feat")
    core, x, y = lax.rem(r, 2), lax.rem(r // 2, SIDE), r // (2 * SIDE)

    def around(value, step):
        return lax.rem(value + step + 2 * SIDE, SIDE)

    def row_of(yy, xx, cc):
        return (yy * SIDE + xx) * 2 + cc

    place = ((x, y), (y, x))
    msg = (msg_a, msg_b)

    def owner(h, u, v, cc):
        return row_of(v, u, cc) if h == 0 else row_of(u, v, cc)

    def near(h, du, dv):
        u, v = place[h]
        return {"rows": owner(h, around(u, du), around(v, dv), core), "feat": z}

    sibling = {"rows": row_of(y, x, 1 - core), "feat": z}

    def along_z(d):
        return lax.rem(z + d, FEAT)

    def send(src, dst, ss, rs, target):
        pltpu.make_async_remote_copy(
            src_ref=src, dst_ref=dst, send_sem=ss, recv_sem=rs, device_id=target, device_id_type=MESH
        ).start()

    def loop(n, body, start=0):
        lax.fori_loop(start, n, lambda i, c: (body(i), c)[1], 0)

    def others(body):
        loop(FEAT, lambda d: body(along_z(d)), 1)

    barrier = pltpu.get_barrier_semaphore()
    partners = [sibling]
    for d in range(1, SIDE):
        partners += [near(0, d, 0), near(1, d, 0)]
    for d in range(1, FEAT):
        partners.append({"rows": r, "feat": along_z(d)})
    for target in partners:
        pl.semaphore_signal(barrier, inc=1, device_id=target, device_id_type=MESH)

    def inc_copy(g, b):
        return pltpu.make_async_copy(
            inc.at[pl.ds(b * GROUP, GROUP), :, pl.ds(g * CHUNK, CHUNK)],
            inc_buf.at[pl.ds((g * BATCHES + b) * GROUP, GROUP)],
            inc_sem.at[g * BATCHES + b],
        )

    for g in range(2):
        for b in range(BATCHES):
            inc_copy(g, b).start()

    lane = lax.broadcasted_iota(jnp.int32, (1, BLOCKS), 1)
    count = jnp.zeros((1, BLOCKS), jnp.int32)
    spots = [jnp.full((1, BLOCKS), NONE, jnp.int32) for _ in range(CAP)]
    for p in range(PAIRS):
        hit = lane == label_ref[p]
        spots = [jnp.where(hit & (count == k), p, spots[k]) for k in range(CAP)]
        count = count + jnp.where(hit, 1, 0)
    tab[...] = jnp.full(tab.shape, NONE, jnp.int32)
    tab_out[...] = jnp.full(tab.shape, NONE, jnp.int32)
    for k in range(CAP):
        tab[k : k + 1, :] = spots[k]
        tab_out[k : k + 1, :] = jnp.where(spots[k] < NONE, spots[k] + PAIRS, NONE)
    own_tab = pltpu.make_async_copy(tab, tab_own, tab_sems.at[0])
    own_tab.start()
    for t in range(feat.shape[1] // TILE):
        tiles[t] = feat[:, t * TILE : (t + 1) * TILE]
    for g in range(2):
        msg[g][NONE] = jnp.zeros((W, CHUNK), bf16)

    pl.semaphore_wait(barrier, len(partners))
    send(tab_out, tab_in, tab_sems.at[1], tab_sems.at[2], sibling)

    tile_count = feat.shape[1] // TILE

    def messages(g):
        def batch(b):
            inc_copy(g, b).wait()
            for k in range(GROUP):
                p = b * GROUP + k
                product = jnp.dot(
                    tiles[lax.rem(doc_ref[p], tile_count)], inc_buf[g * PAIRS + p], preferred_element_type=f32
                )
                msg[g][p] = (message_scale * product).astype(bf16)
            send(
                msg[g].at[pl.ds(b * GROUP, GROUP)], msg[g].at[pl.ds(PAIRS + b * GROUP, GROUP)],
                sib_ss.at[g], sib_rs.at[g * BATCHES + b], sibling,
            )

        loop(BATCHES, batch)

    def pair_messages_in(g):
        def one(b):
            wait(msg[g].at[pl.ds(PAIRS + b * GROUP, GROUP)], sib_rs.at[g * BATCHES + b])

        loop(BATCHES, one)

    def block_id(h, u, v, j, cc):
        return owner(h, u, v, cc) * LB + 2 * h + j

    def part(g, h, du, dv, j):
        u, v = place[h]
        block = block_id(h, around(u, du), around(v, dv), j, core)
        total = msg[g][tab_own[0, block]].astype(f32)
        for k in range(1, CAP):
            total = total + msg[g][tab_own[k, block]].astype(f32)
        for k in range(CAP):
            total = total + msg[g][tab_sib[k, block]].astype(f32)
        return total

    def slot(g, a, i, h, j):
        return (((a * 2 + g) * SIDE + i) * 2 + h) * 2 + j

    def far(g):
        def one(i):
            for h in range(2):
                for j in range(2):
                    k = slot(g, 0, i, h, j)
                    s1_send[k] = part(g, h, 2, offset(i), j).astype(bf16)
                    send(s1_send.at[k], s1_recv.at[k], s1_ss, s1_rs.at[k], near(h, 1 - 2 * j, 0))

        loop(SIDE, one)

    def close(g, passed):
        def one(i):
            for h in range(2):
                for way in range(2):
                    du = 1 - 2 * way
                    j = way if passed else 1 - way
                    k = slot(g, way, i, h, j)
                    total = part(g, h, du, offset(i), j)
                    if passed:
                        q = slot(g, 0, i, h, j)
                        wait(s1_recv.at[q], s1_rs.at[q])
                        total = total + s1_recv[q].astype(f32)
                    s2_send[k] = total.astype(bf16)
                    send(s2_send.at[k], s2_recv.at[k], s2_ss, s2_rs.at[k], near(h, du, 0))

        loop(SIDE, one)

    def column(g, i, h, j):
        total = part(g, h, 0, offset(i), j)
        for way in (1 - j, j):
            k = slot(g, way, i, h, j)
            wait(s2_recv.at[k], s2_rs.at[k])
            total = total + s2_recv[k].astype(f32)
        return total

    def four(way, h, j):
        return (way * 2 + h) * 2 + j

    def second_axis_sums(g):
        for h in range(2):
            for j in range(2):
                k = 4 * g + 2 * h + j
                t1_send[k] = column(g, 0, h, j).astype(bf16)
                send(t1_send.at[k], t1_recv.at[k], t_ss.at[0], t1_rs.at[k], near(h, 0, 1 - 2 * j))
        for passed in (False, True):
            for way in range(2):
                for h in range(2):
                    j = way if passed else 1 - way
                    k = 8 * g + four(way, h, j)
                    total = column(g, 1 + way, h, j)
                    if passed:
                        q = 4 * g + 2 * h + j
                        wait(t1_recv.at[q], t1_rs.at[q])
                        total = total + t1_recv[q].astype(f32)
                    t2_send[k] = total.astype(bf16)
                    send(t2_send.at[k], t2_recv.at[k], t_ss.at[1], t2_rs.at[k], near(h, 0, 1 - 2 * way))

    own_rows = pl.ds(pl.multiple_of(z * W, W), W)

    def rows_at(zz):
        return pl.ds(pl.multiple_of(zz * W, W), W)

    def lanes_in_block(zz, base=0):
        return pl.ds(pl.multiple_of(base + lax.rem(zz, 2) * PART, PART), PART)

    def lanes_in_all(zz, g):
        return pl.ds(pl.multiple_of((zz // 2) * TILE + g * CHUNK + lax.rem(zz, 2) * PART, PART), PART)

    def group_lanes(g):
        return pl.ds(g * PART, PART)

    def to(zz):
        return {"rows": r, "feat": zz}

    def finish_sums(g):
        for h in range(2):
            for j in range(2):
                total = column(g, 3, h, j)
                for way in (1 - j, j):
                    k = 8 * g + four(way, h, j)
                    wait(t2_recv.at[k], t2_rs.at[k])
                    total = total + t2_recv[k].astype(f32)
                summed[g * LB + 2 * h + j] = total.astype(bf16)

        def one(zz):
            send(summed.at[g * LB + zz // 2, :, lanes_in_block(zz)], xin.at[own_rows, group_lanes(g)],
                 z_ss.at[2], x_rs.at[g * FEAT + z], to(zz))

        others(one)
        xin[own_rows, group_lanes(g)] = summed[g * LB + z // 2, :, lanes_in_block(z)]

    def background():
        def one(zz):
            send(weight, wfull.at[own_rows, :], z_ss.at[0], w_rs.at[z], to(zz))
            for g in range(2):
                send(cot.at[:, lanes_in_all(zz, g)], cot_in.at[own_rows, group_lanes(g)],
                     z_ss.at[1], cot_rs.at[g * FEAT + z], to(zz))

        others(one)
        wfull[own_rows, :] = weight[...]
        for g in range(2):
            cot_in[own_rows, group_lanes(g)] = cot[:, lanes_in_all(z, g)]

    own_copies = []

    def mix(g):
        if g == 0:
            others(lambda zz: wait(wfull.at[rows_at(zz), :], w_rs.at[zz]))
            for gg in range(2):
                others(lambda zz: wait(cot_in.at[rows_at(zz), group_lanes(gg)], cot_rs.at[gg * FEAT + zz]))
        others(lambda zz: wait(xin.at[rows_at(zz), group_lanes(g)], x_rs.at[g * FEAT + zz]))

        def forth(o):
            rows = pl.ds(pl.multiple_of(o * CHUNK, CHUNK), CHUNK)
            mixed = lax.dot_general(
                wfull[:, rows], xin[:, group_lanes(g)], (((0,), (0,)), ((), ())), preferred_element_type=f32
            )
            gate = jax.nn.sigmoid(mixed)
            act_buf[rows, group_lanes(g)] = (mixed * gate).astype(bf16)
            slope = gate * (1.0 + mixed * (1.0 - gate))
            gm_buf[rows, group_lanes(g)] = (cot_in[rows, group_lanes(g)].astype(f32) * slope).astype(bf16)

        loop(D // CHUNK, forth)

        def back(o):
            rows = pl.ds(pl.multiple_of(o * CHUNK, CHUNK), CHUNK)
            gmt_buf[rows, group_lanes(g)] = jnp.dot(
                wfull[rows, :], gm_buf[:, group_lanes(g)], preferred_element_type=f32
            ).astype(bf16)

        loop(D // CHUNK, back)
        mine = grads.at[g, r * LB + z // 2, :, lanes_in_block(z)]
        others(lambda zz: send(gmt_buf.at[rows_at(zz), group_lanes(g)], mine, z_ss.at[3], gz_rs.at[g * FEAT + z], to(zz)))
        own = pltpu.make_async_copy(gmt_buf.at[own_rows, group_lanes(g)], mine, local_sem.at[g])
        own.start()
        there = act_out.at[:, lanes_in_all(z, g)]
        others(lambda zz: send(act_buf.at[rows_at(zz), group_lanes(g)], there, z_ss.at[4], act_rs.at[g * FEAT + z], to(zz)))
        own_act = pltpu.make_async_copy(act_buf.at[own_rows, group_lanes(g)], there, local_sem.at[2 + g])
        own_act.start()
        own_copies.append((own, own_act))

    def share(g, block):
        send(grads.at[g, block], grads.at[g, block], ag_ss, pair_rs, sibling)

    def pass_on(g, block, rs, target):
        send(grads.at[g, block], grads.at[g, block], ag_ss, rs, target)

    def at(h, du, dv, j):
        u, v = place[h]
        return block_id(h, around(u, du), around(v, dv), j, core)

    def second_axis(g, n, du, h, j):
        for way in range(2):
            pass_on(g, at(h, du, 0, j), q1_rs.at[g * 32 + n * 8 + four(way, h, j)], near(h, 0, 1 - 2 * way))

    def gather_own(g):
        own_copies[g][0].wait()
        others(lambda zz: wait(grads.at[g, r * LB + zz // 2, :, lanes_in_block(zz)], gz_rs.at[g * FEAT + zz]))
        for way in range(2):
            for h in range(2):
                for j in (way, 1 - way):
                    pass_on(g, at(h, 0, 0, j), p1_rs.at[8 * g + four(way, h, j)], near(h, 1 - 2 * way, 0))
        for h in range(2):
            for j in range(2):
                second_axis(g, 0, 0, h, j)
                share(g, at(h, 0, 0, j))

    def gather_near(g):
        for turn in range(2):
            for way in range(2):
                j = way if turn == 0 else 1 - way
                du = 2 * way - 1
                for h in range(2):
                    block = at(h, du, 0, j)
                    wait(grads.at[g, block], p1_rs.at[8 * g + four(way, h, j)])
                    if j == way:
                        pass_on(g, block, p2_rs.at[4 * g + 2 * h + way], near(h, 1 - 2 * way, 0))
                    second_axis(g, 1 + way, du, h, j)
                    share(g, block)

    def gather_far(g):
        for h in range(2):
            for j in range(2):
                block = at(h, 2, 0, j)
                wait(grads.at[g, block], p2_rs.at[4 * g + 2 * h + j])
                second_axis(g, 3, 2, h, j)
                share(g, block)

    offs = (0, -1, 1, 2)

    def take(g, n):
        for way in range(2):
            for h in range(2):
                for j in (way, 1 - way):
                    block = at(h, offs[n], 2 * way - 1, j)
                    wait(grads.at[g, block], q1_rs.at[g * 32 + n * 8 + four(way, h, j)])
                    if j == way:
                        pass_on(g, block, q2_rs.at[g * 16 + n * 4 + 2 * h + way], near(h, 0, 1 - 2 * way))
                    share(g, block)

    def take_last(g):
        for n in range(4):
            for h in range(2):
                for j in range(2):
                    block = at(h, offs[n], 2, j)
                    wait(grads.at[g, block], q2_rs.at[g * 16 + n * 4 + 2 * h + j])
                    share(g, block)

    HALF = W // 2

    def slab(s, cc):
        return pl.ds(pl.multiple_of(s * W + cc * HALF, HALF), HALF)

    def weight_terms():
        def one(s):
            rows = pl.ds(pl.multiple_of(s * CHUNK, CHUNK), CHUNK)
            wgp[rows, :] = lax.dot_general(
                xin[rows, :], gm_buf[...], (((1,), (1,)), ((), ())), preferred_element_type=f32
            )

        loop(D // CHUNK, one)
        loop(FEAT, lambda s: send(wgp.at[slab(s, 1 - core), :], wgc_recv.at[s], wg_ss.at[0], wgc_rs.at[s], sibling))

    def weight_to_z():
        def one(zz):
            wait(wgc_recv.at[zz], wgc_rs.at[zz])
            wgz_send[zz] = (wgp[slab(zz, core), :] + wgc_recv[zz]).astype(bf16)
            send(wgz_send.at[zz], wgz_recv.at[z], wg_ss.at[1], wgz_rs.at[z], to(zz))

        others(one)
        wait(wgc_recv.at[z], wgc_rs.at[z])

    def weight_to_x():
        wg_half[...] = wgp[slab(z, core), :] + wgc_recv[z]

        def one(zz):
            wait(wgz_recv.at[zz], wgz_rs.at[zz])
            wg_half[...] += wgz_recv[zz].astype(f32)

        others(one)
        for t in range(36):
            a, b = t // 6, t % 6
            wx_send[t // 9, t % 9] = wg_half[8 * a : 8 * a + 8, 128 * b : 128 * b + 128]
        for d in range(1, SIDE):
            xx = around(x, d)
            send(wx_send.at[xx], wx_recv.at[x], wg_ss.at[2], wx_rs.at[x], near(0, d, 0))

    def weight_to_y():
        total = wx_send[x]
        for d in range(1, SIDE):
            xx = around(x, d)
            wait(wx_recv.at[xx], wx_rs.at[xx])
            total = total + wx_recv[xx]
        wy_send[...] = total
        wy_recv[y] = total
        for d in range(1, SIDE):
            send(wy_send, wy_recv.at[y], wg_ss.at[3], wy_rs.at[y], near(1, d, 0))

    def weight_back_x():
        for d in range(1, SIDE):
            yy = around(y, d)
            wait(wy_recv.at[yy], wy_rs.at[yy])
        total = (wy_recv[0] + wy_recv[1]) + (wy_recv[2] + wy_recv[3])
        wf_send[...] = total
        wf_recv[x] = total
        for d in range(1, SIDE):
            send(wf_send, wf_recv.at[x], wg_ss.at[4], wf_rs.at[x], near(0, d, 0))

    mine = pl.ds(pl.multiple_of(core * HALF, HALF), HALF)
    other = pl.ds(pl.multiple_of((1 - core) * HALF, HALF), HALF)
    own_wg = pltpu.make_async_copy(wg_half, wg_out.at[mine, :], local_sem.at[4])

    def weight_done():
        for d in range(1, SIDE):
            xx = around(x, d)
            wait(wf_recv.at[xx], wf_rs.at[xx])
        for t in range(36):
            a, b = t // 6, t % 6
            wg_half[8 * a : 8 * a + 8, 128 * b : 128 * b + 128] = wf_recv[t // 9, t % 9]
        send(wg_half, wg_out.at[mine, :], wg_ss.at[5], wl_rs, sibling)
        own_wg.start()

    background()
    messages(0)
    wait(tab_in, tab_sems.at[2])
    sib_tab = pltpu.make_async_copy(tab_in, tab_sib, tab_sems.at[3])
    sib_tab.start()
    own_tab.wait()
    sib_tab.wait()
    pair_messages_in(0)
    far(0)
    close(0, False)
    messages(1)
    close(0, True)
    pair_messages_in(1)
    far(1)
    second_axis_sums(0)
    close(1, False)
    finish_sums(0)
    close(1, True)
    mix(0)
    second_axis_sums(1)
    gather_own(0)
    finish_sums(1)
    gather_near(0)
    mix(1)
    gather_far(0)
    weight_terms()
    take(0, 0)
    take(0, 1)
    gather_own(1)
    weight_to_z()
    take(0, 2)
    take(0, 3)
    gather_near(1)
    take_last(0)
    gather_far(1)
    weight_to_x()
    take(1, 0)
    weight_to_y()
    take(1, 1)
    weight_back_x()
    take(1, 2)
    weight_done()
    take(1, 3)
    take_last(1)

    own_wg.wait()
    wait(wg_out.at[other, :], wl_rs)
    for g in range(2):
        own_copies[g][1].wait()
        others(lambda zz: wait(act_out.at[:, lanes_in_all(zz, g)], act_rs.at[g * FEAT + zz]))
    for g in range(2):
        wait(msg[g].at[pl.ds(0, PAIRS)], sib_ss.at[g])
    wait(grads.at[:, pl.ds(0, 64)], pair_rs)
    wait(grads.at[:, pl.ds(0, 124)], ag_ss)
    wait(tab_out, tab_sems.at[1])
    wait(s1_send, s1_ss)
    wait(s2_send, s2_ss)
    wait(t1_send, t_ss.at[0])
    wait(t2_send, t_ss.at[1])
    seven = pl.ds(0, (FEAT - 1) * W)
    wait(wfull.at[seven, :], z_ss.at[0])
    for k in range(1, 5):
        wait(cot_in.at[seven, :], z_ss.at[k])
    wait(wgc_recv, wg_ss.at[0])
    wait(wgz_send.at[pl.ds(0, FEAT - 1)], wg_ss.at[1])
    for k in (2, 3, 4):
        wait(wx_send.at[pl.ds(0, SIDE - 1)], wg_ss.at[k])
    wait(wg_half, wg_ss.at[5])


def exchange(doc, label, feat, inc, weight, cot):
    dma = pltpu.SemaphoreType.DMA
    block = (W, CHUNK)
    vmem = pltpu.VMEM
    smem_spec = pl.BlockSpec(memory_space=pltpu.SMEM)
    any_spec = pl.BlockSpec(memory_space=pl.ANY)
    vmem_spec = pl.BlockSpec(memory_space=pltpu.VMEM)
    table = ((8, BLOCKS), jnp.int32)
    return pl.pallas_call(
        exchange_kernel,
        in_specs=[smem_spec, smem_spec, vmem_spec, any_spec, vmem_spec, vmem_spec],
        out_specs=[any_spec] * 3,
        out_shape=[
            jax.ShapeDtypeStruct(cot.shape, bf16),
            jax.ShapeDtypeStruct((W, D), f32),
            jax.ShapeDtypeStruct((2, BLOCKS, *block), bf16),
        ],
        scratch_shapes=[
            vmem((feat.shape[1] // TILE, W, TILE), bf16),
            vmem((2 * PAIRS, TILE, CHUNK), bf16), vmem((NONE + 1, *block), bf16), vmem((NONE + 1, *block), bf16),
            vmem(*table), vmem(*table), vmem(*table), pltpu.SMEM(*table), pltpu.SMEM(*table),
            vmem((32, *block), bf16), vmem((32, *block), bf16),
            vmem((64, *block), bf16), vmem((64, *block), bf16),
            vmem((8, *block), bf16), vmem((8, *block), bf16),
            vmem((16, *block), bf16), vmem((16, *block), bf16),
            vmem((2 * LB, *block), bf16),
            vmem((D, CHUNK), bf16), vmem((D, D), bf16), vmem((D, CHUNK), bf16),
            vmem((D, CHUNK), bf16), vmem((D, CHUNK), bf16), vmem((D, CHUNK), bf16),
            vmem((D, D), f32), vmem((FEAT, W // 2, D), f32),
            vmem((FEAT, W // 2, D), bf16), vmem((FEAT, W // 2, D), bf16),
            vmem((SIDE, 9, 8, 128), f32), vmem((SIDE, 9, 8, 128), f32),
            vmem((9, 8, 128), f32), vmem((SIDE, 9, 8, 128), f32),
            vmem((9, 8, 128), f32), vmem((SIDE, 9, 8, 128), f32),
            vmem((W // 2, D), f32),
            dma((2 * BATCHES,)), dma((4,)), dma((2,)), dma((2 * BATCHES,)),
            dma, dma((32,)), dma, dma((64,)), dma((2,)), dma((8,)), dma((16,)),
            dma((5,)), dma((2 * FEAT,)), dma((FEAT,)), dma((2 * FEAT,)), dma((2 * FEAT,)), dma((2 * FEAT,)), dma((5,)),
            dma, dma((16,)), dma((8,)), dma((64,)), dma((32,)), dma,
            dma((6,)), dma((FEAT,)), dma((FEAT,)), dma((SIDE,)), dma((SIDE,)), dma((SIDE,)), dma,
        ],
        compiler_params=pltpu.CompilerParams(
            collective_id=0, has_side_effects=True, vmem_limit_bytes=VMEM_LIMIT
        ),
    )(doc, label, feat, inc, weight, cot)


def local(features, pair_doc, pair_label, incidence, weight, cotangent):
    act, weight_grad, grads = exchange(
        pair_doc, pair_label, features.T, incidence, weight, cotangent.T
    )
    feature_grad = backward_pairs(pair_doc, pair_label, grads, incidence, features.shape[0])
    return act.T, weight_grad, feature_grad.T


def solution(mesh):
    return jax.shard_map(
        local,
        mesh=mesh,
        in_specs=(
            P("rows", "feat"),
            P("rows"),
            P("rows"),
            P("rows", None, None),
            P("feat", None),
            P("rows", "feat"),
        ),
        out_specs=(P("rows", "feat"), P("feat", None), P("rows", "feat")),
        check_vma=False,
    )
```

```python
import functools

import jax
import jax.numpy as jnp
from jax import lax
from jax.experimental import pallas as pl
from jax.experimental.pallas import tpu as pltpu
from jax.sharding import PartitionSpec as P

MESH = pl.DeviceIdType.MESH
message_scale = 0.0625

SIDE = 4
FEAT = 8
LB = 4
CAP = 3
TILE = 512
PAIRS = 24
W = 96
D = 768
GROUP = 4
BLOCKS = 128
CHUNK = 256
PART = 128
BATCHES = PAIRS // GROUP
NONE = 2 * PAIRS
VMEM_LIMIT = 60 * 1024 * 1024

f32, bf16 = jnp.float32, jnp.bfloat16


def wait(ref, sem):
    pltpu.make_async_copy(ref, ref, sem).wait()


def offset(i):
    return 2 - i + 3 * (i // 2) - 2 * (i // 3)


def exchange_kernel(
    doc_ref, label_ref, feat, inc, weight, cot,
    act_out, wg_out, fg_out,
    grads_a, grads_b, fg_acc,
    tiles, inc_buf, msg_a, msg_b, tab, tab_out, tab_in, tab_own, tab_sib,
    s1_send, s1_recv, s2_send, s2_recv, t1_send, t1_recv, t2_send, t2_recv,
    summed, xin, wfull, cot_in, act_buf, gm_buf, gmt_buf,
    wgp, wgc_recv, wgz_send, wgz_recv, wx_send, wx_recv, wy_send, wy_recv, wf_send, wf_recv, wg_half,
    inc_sem, tab_sems, sib_ss, sib_rs, s1_ss, s1_rs, s2_ss, s2_rs, t_ss, t1_rs, t2_rs,
    z_ss, x_rs, w_rs, cot_rs, act_rs, gz_rs, local_sem,
    ag_ss, p1_rs, p2_rs, q1_rs, q2_rs, pair_rs,
    wg_ss, wgc_rs, wgz_rs, wx_rs, wy_rs, wf_rs, wl_rs,
):
    r, z = lax.axis_index("rows"), lax.axis_index("feat")
    core, x, y = lax.rem(r, 2), lax.rem(r // 2, SIDE), r // (2 * SIDE)

    def around(value, step):
        return lax.rem(value + step + 2 * SIDE, SIDE)

    def row_of(yy, xx, cc):
        return (yy * SIDE + xx) * 2 + cc

    place = ((x, y), (y, x))
    msg = (msg_a, msg_b)
    grads = (grads_a, grads_b)

    def owner(h, u, v, cc):
        return row_of(v, u, cc) if h == 0 else row_of(u, v, cc)

    def near(h, du, dv):
        u, v = place[h]
        return {"rows": owner(h, around(u, du), around(v, dv), core), "feat": z}

    sibling = {"rows": row_of(y, x, 1 - core), "feat": z}

    def along_z(d):
        return lax.rem(z + d, FEAT)

    def send(src, dst, ss, rs, target):
        pltpu.make_async_remote_copy(
            src_ref=src, dst_ref=dst, send_sem=ss, recv_sem=rs, device_id=target, device_id_type=MESH
        ).start()

    def loop(n, body, start=0):
        lax.fori_loop(start, n, lambda i, c: (body(i), c)[1], 0)

    def others(body):
        loop(FEAT, lambda d: body(along_z(d)), 1)

    barrier = pltpu.get_barrier_semaphore()
    partners = [sibling]
    for d in range(1, SIDE):
        partners += [near(0, d, 0), near(1, d, 0)]
    for d in range(1, FEAT):
        partners.append({"rows": r, "feat": along_z(d)})
    for target in partners:
        pl.semaphore_signal(barrier, inc=1, device_id=target, device_id_type=MESH)

    def inc_copy(g, b):
        return pltpu.make_async_copy(
            inc.at[pl.ds(b * GROUP, GROUP), :, pl.ds(g * CHUNK, CHUNK)],
            inc_buf.at[pl.ds((g * BATCHES + b) * GROUP, GROUP)],
            inc_sem.at[g * BATCHES + b],
        )

    for g in range(2):
        for b in range(BATCHES):
            inc_copy(g, b).start()

    lane = lax.broadcasted_iota(jnp.int32, (1, BLOCKS), 1)
    count = jnp.zeros((1, BLOCKS), jnp.int32)
    spots = [jnp.full((1, BLOCKS), NONE, jnp.int32) for _ in range(CAP)]
    for p in range(PAIRS):
        hit = lane == label_ref[p]
        spots = [jnp.where(hit & (count == k), p, spots[k]) for k in range(CAP)]
        count = count + jnp.where(hit, 1, 0)
    tab[...] = jnp.full(tab.shape, NONE, jnp.int32)
    tab_out[...] = jnp.full(tab.shape, NONE, jnp.int32)
    for k in range(CAP):
        tab[k : k + 1, :] = spots[k]
        tab_out[k : k + 1, :] = jnp.where(spots[k] < NONE, spots[k] + PAIRS, NONE)
    own_tab = pltpu.make_async_copy(tab, tab_own, tab_sems.at[0])
    own_tab.start()
    for t in range(feat.shape[1] // TILE):
        tiles[t] = feat[:, t * TILE : (t + 1) * TILE]
    for g in range(2):
        msg[g][NONE] = jnp.zeros((W, CHUNK), bf16)

    pl.semaphore_wait(barrier, len(partners))
    send(tab_out, tab_in, tab_sems.at[1], tab_sems.at[2], sibling)

    tile_count = feat.shape[1] // TILE

    def messages(g):
        def batch(b):
            inc_copy(g, b).wait()
            for k in range(GROUP):
                p = b * GROUP + k
                product = jnp.dot(
                    tiles[lax.rem(doc_ref[p], tile_count)], inc_buf[g * PAIRS + p], preferred_element_type=f32
                )
                msg[g][p] = (message_scale * product).astype(bf16)
            send(
                msg[g].at[pl.ds(b * GROUP, GROUP)], msg[g].at[pl.ds(PAIRS + b * GROUP, GROUP)],
                sib_ss.at[g], sib_rs.at[g * BATCHES + b], sibling,
            )

        loop(BATCHES, batch)

    def pair_messages_in(g):
        def one(b):
            wait(msg[g].at[pl.ds(PAIRS + b * GROUP, GROUP)], sib_rs.at[g * BATCHES + b])

        loop(BATCHES, one)

    def block_id(h, u, v, j, cc):
        return owner(h, u, v, cc) * LB + 2 * h + j

    def part(g, h, du, dv, j):
        u, v = place[h]
        block = block_id(h, around(u, du), around(v, dv), j, core)
        total = msg[g][tab_own[0, block]].astype(f32)
        for k in range(1, CAP):
            total = total + msg[g][tab_own[k, block]].astype(f32)
        for k in range(CAP):
            total = total + msg[g][tab_sib[k, block]].astype(f32)
        return total

    def slot(g, a, i, h, j):
        return (((a * 2 + g) * SIDE + i) * 2 + h) * 2 + j

    def far(g):
        def one(i):
            for h in range(2):
                for j in range(2):
                    k = slot(g, 0, i, h, j)
                    s1_send[k] = part(g, h, 2, offset(i), j).astype(bf16)
                    send(s1_send.at[k], s1_recv.at[k], s1_ss, s1_rs.at[k], near(h, 1 - 2 * j, 0))

        loop(SIDE, one)

    def close(g, passed):
        def one(i):
            for h in range(2):
                for way in range(2):
                    du = 1 - 2 * way
                    j = way if passed else 1 - way
                    k = slot(g, way, i, h, j)
                    total = part(g, h, du, offset(i), j)
                    if passed:
                        q = slot(g, 0, i, h, j)
                        wait(s1_recv.at[q], s1_rs.at[q])
                        total = total + s1_recv[q].astype(f32)
                    s2_send[k] = total.astype(bf16)
                    send(s2_send.at[k], s2_recv.at[k], s2_ss, s2_rs.at[k], near(h, du, 0))

        loop(SIDE, one)

    def column(g, i, h, j):
        total = part(g, h, 0, offset(i), j)
        for way in (1 - j, j):
            k = slot(g, way, i, h, j)
            wait(s2_recv.at[k], s2_rs.at[k])
            total = total + s2_recv[k].astype(f32)
        return total

    def four(way, h, j):
        return (way * 2 + h) * 2 + j

    def second_axis_sums(g):
        for h in range(2):
            for j in range(2):
                k = 4 * g + 2 * h + j
                t1_send[k] = column(g, 0, h, j).astype(bf16)
                send(t1_send.at[k], t1_recv.at[k], t_ss.at[0], t1_rs.at[k], near(h, 0, 1 - 2 * j))
        for passed in (False, True):
            for way in range(2):
                for h in range(2):
                    j = way if passed else 1 - way
                    k = 8 * g + four(way, h, j)
                    total = column(g, 1 + way, h, j)
                    if passed:
                        q = 4 * g + 2 * h + j
                        wait(t1_recv.at[q], t1_rs.at[q])
                        total = total + t1_recv[q].astype(f32)
                    t2_send[k] = total.astype(bf16)
                    send(t2_send.at[k], t2_recv.at[k], t_ss.at[1], t2_rs.at[k], near(h, 0, 1 - 2 * way))

    own_rows = pl.ds(pl.multiple_of(z * W, W), W)

    def rows_at(zz):
        return pl.ds(pl.multiple_of(zz * W, W), W)

    def lanes_in_block(zz, base=0):
        return pl.ds(pl.multiple_of(base + lax.rem(zz, 2) * PART, PART), PART)

    def lanes_in_all(zz, g):
        return pl.ds(pl.multiple_of((zz // 2) * TILE + g * CHUNK + lax.rem(zz, 2) * PART, PART), PART)

    def group_lanes(g):
        return pl.ds(g * PART, PART)

    def to(zz):
        return {"rows": r, "feat": zz}

    def finish_sums(g):
        for h in range(2):
            for j in range(2):
                total = column(g, 3, h, j)
                for way in (1 - j, j):
                    k = 8 * g + four(way, h, j)
                    wait(t2_recv.at[k], t2_rs.at[k])
                    total = total + t2_recv[k].astype(f32)
                summed[g * LB + 2 * h + j] = total.astype(bf16)

        def one(zz):
            send(summed.at[g * LB + zz // 2, :, lanes_in_block(zz)], xin.at[own_rows, group_lanes(g)],
                 z_ss.at[2], x_rs.at[g * FEAT + z], to(zz))

        others(one)
        xin[own_rows, group_lanes(g)] = summed[g * LB + z // 2, :, lanes_in_block(z)]

    def pass_weight(slab, step):
        rows = rows_at(slab)
        send(wfull.at[rows, :], wfull.at[rows, :], z_ss.at[0], w_rs.at[slab], to(lax.rem(z + step + FEAT, FEAT)))

    def weight_start():
        wfull[own_rows, :] = weight[...]
        pass_weight(z, 1)
        pass_weight(z, -1)

    def weight_forward(n):
        below, above = lax.rem(z - n + FEAT, FEAT), lax.rem(z + n, FEAT)
        wait(wfull.at[rows_at(below), :], w_rs.at[below])
        if n < FEAT // 2:
            pass_weight(below, 1)
            wait(wfull.at[rows_at(above), :], w_rs.at[above])
            if n < FEAT // 2 - 1:
                pass_weight(above, -1)

    def spread_cotangent():
        def one(zz):
            for g in range(2):
                send(cot.at[:, lanes_in_all(zz, g)], cot_in.at[own_rows, group_lanes(g)],
                     z_ss.at[1], cot_rs.at[g * FEAT + z], to(zz))

        others(one)
        for g in range(2):
            cot_in[own_rows, group_lanes(g)] = cot[:, lanes_in_all(z, g)]

    own_copies = []

    def mix(g):
        if g == 0:
            weight_forward(FEAT // 2)
            for gg in range(2):
                others(lambda zz: wait(cot_in.at[rows_at(zz), group_lanes(gg)], cot_rs.at[gg * FEAT + zz]))
        others(lambda zz: wait(xin.at[rows_at(zz), group_lanes(g)], x_rs.at[g * FEAT + zz]))

        def forth(o):
            rows = pl.ds(pl.multiple_of(o * CHUNK, CHUNK), CHUNK)
            mixed = lax.dot_general(
                wfull[:, rows], xin[:, group_lanes(g)], (((0,), (0,)), ((), ())), preferred_element_type=f32
            )
            gate = jax.nn.sigmoid(mixed)
            act_buf[rows, group_lanes(g)] = (mixed * gate).astype(bf16)
            slope = gate * (1.0 + mixed * (1.0 - gate))
            gm_buf[rows, group_lanes(g)] = (cot_in[rows, group_lanes(g)].astype(f32) * slope).astype(bf16)

        loop(D // CHUNK, forth)

        def back(o):
            rows = pl.ds(pl.multiple_of(o * CHUNK, CHUNK), CHUNK)
            gmt_buf[rows, group_lanes(g)] = jnp.dot(
                wfull[rows, :], gm_buf[:, group_lanes(g)], preferred_element_type=f32
            ).astype(bf16)

        loop(D // CHUNK, back)
        mine = grads[g].at[r * LB + z // 2, :, lanes_in_block(z)]
        others(lambda zz: send(gmt_buf.at[rows_at(zz), group_lanes(g)], mine, z_ss.at[3], gz_rs.at[g * FEAT + z], to(zz)))
        own = pltpu.make_async_copy(gmt_buf.at[own_rows, group_lanes(g)], mine, local_sem.at[g])
        own.start()
        own_copies.append(own)

    own_acts = []

    def give_act(g):
        there = act_out.at[:, lanes_in_all(z, g)]
        others(lambda zz: send(act_buf.at[rows_at(zz), group_lanes(g)], there, z_ss.at[4], act_rs.at[g * FEAT + z], to(zz)))
        own_act = pltpu.make_async_copy(act_buf.at[own_rows, group_lanes(g)], there, local_sem.at[2 + g])
        own_act.start()
        own_acts.append(own_act)

    def share(g, block):
        send(grads[g].at[block], grads[g].at[block], ag_ss.at[g], pair_rs.at[g], sibling)

    def pass_on(g, block, rs, target):
        send(grads[g].at[block], grads[g].at[block], ag_ss.at[g], rs, target)

    def at(h, du, dv, j):
        u, v = place[h]
        return block_id(h, around(u, du), around(v, dv), j, core)

    def second_axis(g, n, du, h, j):
        for way in range(2):
            pass_on(g, at(h, du, 0, j), q1_rs.at[g * 32 + n * 8 + four(way, h, j)], near(h, 0, 1 - 2 * way))

    def gather_own(g):
        own_copies[g].wait()
        others(lambda zz: wait(grads[g].at[r * LB + zz // 2, :, lanes_in_block(zz)], gz_rs.at[g * FEAT + zz]))
        for way in range(2):
            for h in range(2):
                for j in (way, 1 - way):
                    pass_on(g, at(h, 0, 0, j), p1_rs.at[8 * g + four(way, h, j)], near(h, 1 - 2 * way, 0))
        for h in range(2):
            for j in range(2):
                second_axis(g, 0, 0, h, j)
                share(g, at(h, 0, 0, j))

    def gather_near(g):
        for turn in range(2):
            for way in range(2):
                j = way if turn == 0 else 1 - way
                du = 2 * way - 1
                for h in range(2):
                    block = at(h, du, 0, j)
                    wait(grads[g].at[block], p1_rs.at[8 * g + four(way, h, j)])
                    if j == way:
                        pass_on(g, block, p2_rs.at[4 * g + 2 * h + way], near(h, 1 - 2 * way, 0))
                    second_axis(g, 1 + way, du, h, j)
                    share(g, block)

    def gather_far(g):
        for h in range(2):
            for j in range(2):
                block = at(h, 2, 0, j)
                wait(grads[g].at[block], p2_rs.at[4 * g + 2 * h + j])
                second_axis(g, 3, 2, h, j)
                share(g, block)

    offs = (0, -1, 1, 2)

    def take(g, n):
        for way in range(2):
            for h in range(2):
                for j in (way, 1 - way):
                    block = at(h, offs[n], 2 * way - 1, j)
                    wait(grads[g].at[block], q1_rs.at[g * 32 + n * 8 + four(way, h, j)])
                    if j == way:
                        pass_on(g, block, q2_rs.at[g * 16 + n * 4 + 2 * h + way], near(h, 0, 1 - 2 * way))
                    share(g, block)

    def take_last(g):
        for n in range(4):
            for h in range(2):
                for j in range(2):
                    block = at(h, offs[n], 2, j)
                    wait(grads[g].at[block], q2_rs.at[g * 16 + n * 4 + 2 * h + j])
                    share(g, block)

    def backward_ready(g):
        wait(grads[g].at[pl.ds(0, 64)], pair_rs.at[g])

    def backward(g, first, last):
        def batch(b):
            left, right = [], []
            for k in range(GROUP):
                p = b * GROUP + k
                grad = grads[g][label_ref[p]]
                tile = lax.rem(doc_ref[p], tile_count)
                left.append(
                    jnp.concatenate(
                        [jnp.where(tile == t, grad, jnp.zeros_like(grad)) for t in range(tile_count)], axis=0
                    )
                )
                right.append(inc_buf[g * PAIRS + p])
            fg_acc[...] += lax.dot_general(
                jnp.concatenate(left, axis=1), jnp.concatenate(right, axis=1),
                (((1,), (1,)), ((), ())), preferred_element_type=f32,
            )

        loop(last, batch, first)

    def backward_done():
        for t in range(tile_count):
            fg_out[:, t * TILE : (t + 1) * TILE] = fg_acc[t * W : (t + 1) * W, :].astype(bf16)

    HALF = W // 2

    def slab(s, cc):
        return pl.ds(pl.multiple_of(s * W + cc * HALF, HALF), HALF)

    def weight_terms():
        def one(s):
            rows = pl.ds(pl.multiple_of(s * CHUNK, CHUNK), CHUNK)
            wgp[rows, :] = lax.dot_general(
                xin[rows, :], gm_buf[...], (((1,), (1,)), ((), ())), preferred_element_type=f32
            )

        loop(D // CHUNK, one)
        loop(FEAT, lambda s: send(wgp.at[slab(s, 1 - core), :], wgc_recv.at[s], wg_ss.at[0], wgc_rs.at[s], sibling))

    def weight_to_z():
        def one(zz):
            wait(wgc_recv.at[zz], wgc_rs.at[zz])
            wgz_send[zz] = (wgp[slab(zz, core), :] + wgc_recv[zz]).astype(bf16)
            send(wgz_send.at[zz], wgz_recv.at[z], wg_ss.at[1], wgz_rs.at[z], to(zz))

        others(one)
        wait(wgc_recv.at[z], wgc_rs.at[z])

    def weight_to_x():
        wg_half[...] = wgp[slab(z, core), :] + wgc_recv[z]

        def one(zz):
            wait(wgz_recv.at[zz], wgz_rs.at[zz])
            wg_half[...] += wgz_recv[zz].astype(f32)

        others(one)
        for t in range(36):
            a, b = t // 6, t % 6
            wx_send[t // 9, t % 9] = wg_half[8 * a : 8 * a + 8, 128 * b : 128 * b + 128]
        for d in range(1, SIDE):
            xx = around(x, d)
            send(wx_send.at[xx], wx_recv.at[x], wg_ss.at[2], wx_rs.at[x], near(0, d, 0))

    def weight_to_y():
        total = wx_send[x]
        for d in range(1, SIDE):
            xx = around(x, d)
            wait(wx_recv.at[xx], wx_rs.at[xx])
            total = total + wx_recv[xx]
        wy_send[...] = total
        wy_recv[y] = total
        for d in range(1, SIDE):
            send(wy_send, wy_recv.at[y], wg_ss.at[3], wy_rs.at[y], near(1, d, 0))

    def weight_back_x():
        for d in range(1, SIDE):
            yy = around(y, d)
            wait(wy_recv.at[yy], wy_rs.at[yy])
        total = (wy_recv[0] + wy_recv[1]) + (wy_recv[2] + wy_recv[3])
        wf_send[...] = total
        wf_recv[x] = total
        for d in range(1, SIDE):
            send(wf_send, wf_recv.at[x], wg_ss.at[4], wf_rs.at[x], near(0, d, 0))

    mine = pl.ds(pl.multiple_of(core * HALF, HALF), HALF)
    other = pl.ds(pl.multiple_of((1 - core) * HALF, HALF), HALF)
    own_wg = pltpu.make_async_copy(wg_half, wg_out.at[mine, :], local_sem.at[4])

    def weight_done():
        for d in range(1, SIDE):
            xx = around(x, d)
            wait(wf_recv.at[xx], wf_rs.at[xx])
        for t in range(36):
            a, b = t // 6, t % 6
            wg_half[8 * a : 8 * a + 8, 128 * b : 128 * b + 128] = wf_recv[t // 9, t % 9]
        send(wg_half, wg_out.at[mine, :], wg_ss.at[5], wl_rs, sibling)
        own_wg.start()

    weight_start()
    messages(0)
    wait(tab_in, tab_sems.at[2])
    sib_tab = pltpu.make_async_copy(tab_in, tab_sib, tab_sems.at[3])
    sib_tab.start()
    own_tab.wait()
    sib_tab.wait()
    pair_messages_in(0)
    weight_forward(1)
    far(0)
    weight_forward(2)
    close(0, False)
    weight_forward(3)
    spread_cotangent()
    messages(1)
    close(0, True)
    pair_messages_in(1)
    far(1)
    second_axis_sums(0)
    close(1, False)
    finish_sums(0)
    close(1, True)
    mix(0)
    second_axis_sums(1)
    gather_own(0)
    finish_sums(1)
    gather_near(0)
    gather_far(0)
    mix(1)
    take(0, 0)
    take(0, 1)
    weight_terms()
    take(0, 2)
    take(0, 3)
    gather_own(1)
    weight_to_z()
    give_act(0)
    give_act(1)
    fg_acc[...] = jnp.zeros_like(fg_acc)
    take_last(0)
    gather_near(1)
    gather_far(1)
    backward_ready(0)
    backward(0, 0, 3)
    take(1, 0)
    backward(0, 3, 6)
    weight_to_x()
    take(1, 1)
    take(1, 2)
    weight_to_y()
    take(1, 3)
    weight_back_x()
    take_last(1)
    weight_done()
    backward_ready(1)
    backward(1, 0, BATCHES)
    backward_done()

    own_wg.wait()
    wait(wg_out.at[other, :], wl_rs)
    for g in range(2):
        own_acts[g].wait()
        others(lambda zz: wait(act_out.at[:, lanes_in_all(zz, g)], act_rs.at[g * FEAT + zz]))
    for g in range(2):
        wait(msg[g].at[pl.ds(0, PAIRS)], sib_ss.at[g])
        wait(grads[g].at[pl.ds(0, 124)], ag_ss.at[g])
    wait(tab_out, tab_sems.at[1])
    wait(s1_send, s1_ss)
    wait(s2_send, s2_ss)
    wait(t1_send, t_ss.at[0])
    wait(t2_send, t_ss.at[1])
    seven = pl.ds(0, (FEAT - 1) * W)
    wait(wfull.at[seven, :], z_ss.at[0])
    for k in range(1, 5):
        wait(cot_in.at[seven, :], z_ss.at[k])
    wait(wgc_recv, wg_ss.at[0])
    wait(wgz_send.at[pl.ds(0, FEAT - 1)], wg_ss.at[1])
    for k in (2, 3, 4):
        wait(wx_send.at[pl.ds(0, SIDE - 1)], wg_ss.at[k])
    wait(wg_half, wg_ss.at[5])


def exchange(doc, label, feat, inc, weight, cot):
    dma = pltpu.SemaphoreType.DMA
    block = (W, CHUNK)
    vmem = pltpu.VMEM
    smem_spec = pl.BlockSpec(memory_space=pltpu.SMEM)
    any_spec = pl.BlockSpec(memory_space=pl.ANY)
    vmem_spec = pl.BlockSpec(memory_space=pltpu.VMEM)
    table = ((8, BLOCKS), jnp.int32)
    return pl.pallas_call(
        exchange_kernel,
        in_specs=[smem_spec, smem_spec, vmem_spec, any_spec, vmem_spec, vmem_spec],
        out_specs=[any_spec, any_spec, vmem_spec],
        out_shape=[
            jax.ShapeDtypeStruct(cot.shape, bf16),
            jax.ShapeDtypeStruct((W, D), f32),
            jax.ShapeDtypeStruct(feat.shape, bf16),
        ],
        scratch_shapes=[
            vmem((BLOCKS, *block), bf16), vmem((BLOCKS, *block), bf16),
            vmem((feat.shape[1] // TILE * W, TILE), f32),
            vmem((feat.shape[1] // TILE, W, TILE), bf16),
            vmem((2 * PAIRS, TILE, CHUNK), bf16), vmem((NONE + 1, *block), bf16), vmem((NONE + 1, *block), bf16),
            vmem(*table), vmem(*table), vmem(*table), pltpu.SMEM(*table), pltpu.SMEM(*table),
            vmem((32, *block), bf16), vmem((32, *block), bf16),
            vmem((64, *block), bf16), vmem((64, *block), bf16),
            vmem((8, *block), bf16), vmem((8, *block), bf16),
            vmem((16, *block), bf16), vmem((16, *block), bf16),
            vmem((2 * LB, *block), bf16),
            vmem((D, CHUNK), bf16), vmem((D, D), bf16), vmem((D, CHUNK), bf16),
            vmem((D, CHUNK), bf16), vmem((D, CHUNK), bf16), vmem((D, CHUNK), bf16),
            vmem((D, D), f32), vmem((FEAT, W // 2, D), f32),
            vmem((FEAT, W // 2, D), bf16), vmem((FEAT, W // 2, D), bf16),
            vmem((SIDE, 9, 8, 128), f32), vmem((SIDE, 9, 8, 128), f32),
            vmem((9, 8, 128), f32), vmem((SIDE, 9, 8, 128), f32),
            vmem((9, 8, 128), f32), vmem((SIDE, 9, 8, 128), f32),
            vmem((W // 2, D), f32),
            dma((2 * BATCHES,)), dma((4,)), dma((2,)), dma((2 * BATCHES,)),
            dma, dma((32,)), dma, dma((64,)), dma((2,)), dma((8,)), dma((16,)),
            dma((5,)), dma((2 * FEAT,)), dma((FEAT,)), dma((2 * FEAT,)), dma((2 * FEAT,)), dma((2 * FEAT,)), dma((5,)),
            dma((2,)), dma((16,)), dma((8,)), dma((64,)), dma((32,)), dma((2,)),
            dma((6,)), dma((FEAT,)), dma((FEAT,)), dma((SIDE,)), dma((SIDE,)), dma((SIDE,)), dma,
        ],
        compiler_params=pltpu.CompilerParams(
            collective_id=0, has_side_effects=True, vmem_limit_bytes=VMEM_LIMIT
        ),
    )(doc, label, feat, inc, weight, cot)


def local(features, pair_doc, pair_label, incidence, weight, cotangent):
    act, weight_grad, feature_grad = exchange(
        pair_doc, pair_label, features.T, incidence, weight, cotangent.T
    )
    return act.T, weight_grad, feature_grad.T


def solution(mesh):
    return jax.shard_map(
        local,
        mesh=mesh,
        in_specs=(
            P("rows", "feat"),
            P("rows"),
            P("rows"),
            P("rows", None, None),
            P("feat", None),
            P("rows", "feat"),
        ),
        out_specs=(P("rows", "feat"), P("feat", None), P("rows", "feat")),
        check_vma=False,
    )
```

```python
import functools

import jax
import jax.numpy as jnp
from jax import lax
from jax.experimental import pallas as pl
from jax.experimental.pallas import tpu as pltpu
from jax.sharding import PartitionSpec as P

MESH = pl.DeviceIdType.MESH
message_scale = 0.0625

SIDE = 4
FEAT = 8
LB = 4
CAP = 3
TILE = 512
PAIRS = 24
W = 96
D = 768
GROUP = 4
BLOCKS = 128
CHUNK = 256
PART = 128
BATCHES = PAIRS // GROUP
NONE = 2 * PAIRS
VMEM_LIMIT = 60 * 1024 * 1024

f32, bf16 = jnp.float32, jnp.bfloat16


def wait(ref, sem):
    pltpu.make_async_copy(ref, ref, sem).wait()


def offset(i):
    return 2 - i + 3 * (i // 2) - 2 * (i // 3)


def exchange_kernel(
    doc_ref, label_ref, feat, inc, weight, cot,
    act_out, wg_out, fg_out,
    grads_a, grads_b, fg_acc,
    tiles, inc_buf, msg_a, msg_b, tab, tab_out, tab_in, tab_own, tab_sib,
    s1_send, s1_recv, s2_send, s2_recv, t1_send, t1_recv, t2_send, t2_recv,
    summed, xin, wfull, cot_in, act_buf, gm_buf, gmt_buf,
    x_pair, gm_pair, wgz_send, wgz_recv, wx_send, wx_recv, wy_send, wy_recv, wf_send, wf_recv, wg_half,
    inc_sem, tab_sems, sib_ss, sib_rs, s1_ss, s1_rs, s2_ss, s2_rs, t_ss, t1_rs, t2_rs,
    z_ss, x_rs, w_rs, cot_rs, act_rs, gz_rs, local_sem,
    ag_ss, p1_rs, p2_rs, q1_rs, q2_rs, pair_rs,
    wg_ss, wgc_rs, wgz_rs, wx_rs, wy_rs, wf_rs, wl_rs,
):
    r, z = lax.axis_index("rows"), lax.axis_index("feat")
    core, x, y = lax.rem(r, 2), lax.rem(r // 2, SIDE), r // (2 * SIDE)

    def around(value, step):
        return lax.rem(value + step + 2 * SIDE, SIDE)

    def row_of(yy, xx, cc):
        return (yy * SIDE + xx) * 2 + cc

    place = ((x, y), (y, x))
    msg = (msg_a, msg_b)
    grads = (grads_a, grads_b)

    def owner(h, u, v, cc):
        return row_of(v, u, cc) if h == 0 else row_of(u, v, cc)

    def near(h, du, dv):
        u, v = place[h]
        return {"rows": owner(h, around(u, du), around(v, dv), core), "feat": z}

    sibling = {"rows": row_of(y, x, 1 - core), "feat": z}

    def along_z(d):
        return lax.rem(z + d, FEAT)

    def send(src, dst, ss, rs, target):
        pltpu.make_async_remote_copy(
            src_ref=src, dst_ref=dst, send_sem=ss, recv_sem=rs, device_id=target, device_id_type=MESH
        ).start()

    def loop(n, body, start=0):
        lax.fori_loop(start, n, lambda i, c: (body(i), c)[1], 0)

    def others(body):
        loop(FEAT, lambda d: body(along_z(d)), 1)

    barrier = pltpu.get_barrier_semaphore()
    partners = [sibling]
    for d in range(1, SIDE):
        partners += [near(0, d, 0), near(1, d, 0)]
    for d in range(1, FEAT):
        partners.append({"rows": r, "feat": along_z(d)})
    for target in partners:
        pl.semaphore_signal(barrier, inc=1, device_id=target, device_id_type=MESH)

    def inc_copy(g, b):
        return pltpu.make_async_copy(
            inc.at[pl.ds(b * GROUP, GROUP), :, pl.ds(g * CHUNK, CHUNK)],
            inc_buf.at[pl.ds((g * BATCHES + b) * GROUP, GROUP)],
            inc_sem.at[g * BATCHES + b],
        )

    for g in range(2):
        for b in range(BATCHES):
            inc_copy(g, b).start()

    lane = lax.broadcasted_iota(jnp.int32, (1, BLOCKS), 1)
    count = jnp.zeros((1, BLOCKS), jnp.int32)
    spots = [jnp.full((1, BLOCKS), NONE, jnp.int32) for _ in range(CAP)]
    for p in range(PAIRS):
        hit = lane == label_ref[p]
        spots = [jnp.where(hit & (count == k), p, spots[k]) for k in range(CAP)]
        count = count + jnp.where(hit, 1, 0)
    tab[...] = jnp.full(tab.shape, NONE, jnp.int32)
    tab_out[...] = jnp.full(tab.shape, NONE, jnp.int32)
    for k in range(CAP):
        tab[k : k + 1, :] = spots[k]
        tab_out[k : k + 1, :] = jnp.where(spots[k] < NONE, spots[k] + PAIRS, NONE)
    own_tab = pltpu.make_async_copy(tab, tab_own, tab_sems.at[0])
    own_tab.start()
    for t in range(feat.shape[1] // TILE):
        tiles[t] = feat[:, t * TILE : (t + 1) * TILE]
    for g in range(2):
        msg[g][NONE] = jnp.zeros((W, CHUNK), bf16)

    pl.semaphore_wait(barrier, len(partners))
    send(tab_out, tab_in, tab_sems.at[1], tab_sems.at[2], sibling)

    tile_count = feat.shape[1] // TILE

    def messages(g):
        def batch(b):
            inc_copy(g, b).wait()
            for k in range(GROUP):
                p = b * GROUP + k
                product = jnp.dot(
                    tiles[lax.rem(doc_ref[p], tile_count)], inc_buf[g * PAIRS + p], preferred_element_type=f32
                )
                msg[g][p] = (message_scale * product).astype(bf16)
            send(
                msg[g].at[pl.ds(b * GROUP, GROUP)], msg[g].at[pl.ds(PAIRS + b * GROUP, GROUP)],
                sib_ss.at[g], sib_rs.at[g * BATCHES + b], sibling,
            )

        loop(BATCHES, batch)

    def pair_messages_in(g):
        def one(b):
            wait(msg[g].at[pl.ds(PAIRS + b * GROUP, GROUP)], sib_rs.at[g * BATCHES + b])

        loop(BATCHES, one)

    def block_id(h, u, v, j, cc):
        return owner(h, u, v, cc) * LB + 2 * h + j

    def part(g, h, du, dv, j):
        u, v = place[h]
        block = block_id(h, around(u, du), around(v, dv), j, core)
        total = msg[g][tab_own[0, block]].astype(f32)
        for k in range(1, CAP):
            total = total + msg[g][tab_own[k, block]].astype(f32)
        for k in range(CAP):
            total = total + msg[g][tab_sib[k, block]].astype(f32)
        return total

    def slot(g, a, i, h, j):
        return (((a * 2 + g) * SIDE + i) * 2 + h) * 2 + j

    def far(g):
        def one(i):
            for h in range(2):
                for j in range(2):
                    k = slot(g, 0, i, h, j)
                    s1_send[k] = part(g, h, 2, offset(i), j).astype(bf16)
                    send(s1_send.at[k], s1_recv.at[k], s1_ss, s1_rs.at[k], near(h, 1 - 2 * j, 0))

        loop(SIDE, one)

    def close(g, passed):
        def one(i):
            for h in range(2):
                for way in range(2):
                    du = 1 - 2 * way
                    j = way if passed else 1 - way
                    k = slot(g, way, i, h, j)
                    total = part(g, h, du, offset(i), j)
                    if passed:
                        q = slot(g, 0, i, h, j)
                        wait(s1_recv.at[q], s1_rs.at[q])
                        total = total + s1_recv[q].astype(f32)
                    s2_send[k] = total.astype(bf16)
                    send(s2_send.at[k], s2_recv.at[k], s2_ss, s2_rs.at[k], near(h, du, 0))

        loop(SIDE, one)

    def column(g, i, h, j):
        total = part(g, h, 0, offset(i), j)
        for way in (1 - j, j):
            k = slot(g, way, i, h, j)
            wait(s2_recv.at[k], s2_rs.at[k])
            total = total + s2_recv[k].astype(f32)
        return total

    def four(way, h, j):
        return (way * 2 + h) * 2 + j

    def second_axis_sums(g):
        for h in range(2):
            for j in range(2):
                k = 4 * g + 2 * h + j
                t1_send[k] = column(g, 0, h, j).astype(bf16)
                send(t1_send.at[k], t1_recv.at[k], t_ss.at[0], t1_rs.at[k], near(h, 0, 1 - 2 * j))
        for passed in (False, True):
            for way in range(2):
                for h in range(2):
                    j = way if passed else 1 - way
                    k = 8 * g + four(way, h, j)
                    total = column(g, 1 + way, h, j)
                    if passed:
                        q = 4 * g + 2 * h + j
                        wait(t1_recv.at[q], t1_rs.at[q])
                        total = total + t1_recv[q].astype(f32)
                    t2_send[k] = total.astype(bf16)
                    send(t2_send.at[k], t2_recv.at[k], t_ss.at[1], t2_rs.at[k], near(h, 0, 1 - 2 * way))

    own_rows = pl.ds(pl.multiple_of(z * W, W), W)

    def rows_at(zz):
        return pl.ds(pl.multiple_of(zz * W, W), W)

    def lanes_in_block(zz, base=0):
        return pl.ds(pl.multiple_of(base + lax.rem(zz, 2) * PART, PART), PART)

    def lanes_in_all(zz, g):
        return pl.ds(pl.multiple_of((zz // 2) * TILE + g * CHUNK + lax.rem(zz, 2) * PART, PART), PART)

    def group_lanes(g):
        return pl.ds(g * PART, PART)

    def to(zz):
        return {"rows": r, "feat": zz}

    def finish_sums(g):
        for h in range(2):
            for j in range(2):
                total = column(g, 3, h, j)
                for way in (1 - j, j):
                    k = 8 * g + four(way, h, j)
                    wait(t2_recv.at[k], t2_rs.at[k])
                    total = total + t2_recv[k].astype(f32)
                summed[g * LB + 2 * h + j] = total.astype(bf16)

        def one(zz):
            send(summed.at[g * LB + zz // 2, :, lanes_in_block(zz)], xin.at[own_rows, group_lanes(g)],
                 z_ss.at[2], x_rs.at[g * FEAT + z], to(zz))

        others(one)
        xin[own_rows, group_lanes(g)] = summed[g * LB + z // 2, :, lanes_in_block(z)]

    half_cols = pl.ds(pl.multiple_of(core * (D // 2), D // 2), D // 2)
    other_cols = pl.ds(pl.multiple_of((1 - core) * (D // 2), D // 2), D // 2)

    def weight_start():
        others(lambda zz: send(weight.at[:, half_cols], wfull.at[own_rows, half_cols], z_ss.at[0], w_rs.at[z], to(zz)))
        wfull[own_rows, :] = weight[...]

    def weight_share():
        def one(zz):
            half = wfull.at[rows_at(zz), half_cols]
            wait(half, w_rs.at[zz])
            send(half, half, z_ss.at[5], w_rs.at[FEAT + zz], sibling)

        others(one)

    def spread_cotangent():
        def one(zz):
            for g in range(2):
                send(cot.at[:, lanes_in_all(zz, g)], cot_in.at[own_rows, group_lanes(g)],
                     z_ss.at[1], cot_rs.at[g * FEAT + z], to(zz))

        others(one)
        for g in range(2):
            cot_in[own_rows, group_lanes(g)] = cot[:, lanes_in_all(z, g)]

    own_copies = []

    def mix(g):
        if g == 0:
            others(lambda zz: wait(wfull.at[rows_at(zz), other_cols], w_rs.at[FEAT + zz]))
            for gg in range(2):
                others(lambda zz: wait(cot_in.at[rows_at(zz), group_lanes(gg)], cot_rs.at[gg * FEAT + zz]))
        others(lambda zz: wait(xin.at[rows_at(zz), group_lanes(g)], x_rs.at[g * FEAT + zz]))

        def forth(o):
            rows = pl.ds(pl.multiple_of(o * CHUNK, CHUNK), CHUNK)
            mixed = lax.dot_general(
                wfull[:, rows], xin[:, group_lanes(g)], (((0,), (0,)), ((), ())), preferred_element_type=f32
            )
            gate = jax.nn.sigmoid(mixed)
            act_buf[rows, group_lanes(g)] = (mixed * gate).astype(bf16)
            slope = gate * (1.0 + mixed * (1.0 - gate))
            gm_buf[rows, group_lanes(g)] = (cot_in[rows, group_lanes(g)].astype(f32) * slope).astype(bf16)

        loop(D // CHUNK, forth)

        def back(o):
            rows = pl.ds(pl.multiple_of(o * CHUNK, CHUNK), CHUNK)
            gmt_buf[rows, group_lanes(g)] = jnp.dot(
                wfull[rows, :], gm_buf[:, group_lanes(g)], preferred_element_type=f32
            ).astype(bf16)

        loop(D // CHUNK, back)
        mine = grads[g].at[r * LB + z // 2, :, lanes_in_block(z)]
        others(lambda zz: send(gmt_buf.at[rows_at(zz), group_lanes(g)], mine, z_ss.at[3], gz_rs.at[g * FEAT + z], to(zz)))
        own = pltpu.make_async_copy(gmt_buf.at[own_rows, group_lanes(g)], mine, local_sem.at[g])
        own.start()
        own_copies.append(own)

    own_acts = []

    def give_act(g):
        there = act_out.at[:, lanes_in_all(z, g)]
        others(lambda zz: send(act_buf.at[rows_at(zz), group_lanes(g)], there, z_ss.at[4], act_rs.at[g * FEAT + z], to(zz)))
        own_act = pltpu.make_async_copy(act_buf.at[own_rows, group_lanes(g)], there, local_sem.at[2 + g])
        own_act.start()
        own_acts.append(own_act)

    def share(g, block):
        send(grads[g].at[block], grads[g].at[block], ag_ss.at[g], pair_rs.at[g], sibling)

    def pass_on(g, block, rs, target):
        send(grads[g].at[block], grads[g].at[block], ag_ss.at[g], rs, target)

    def at(h, du, dv, j):
        u, v = place[h]
        return block_id(h, around(u, du), around(v, dv), j, core)

    def second_axis(g, n, du, h, j):
        for way in range(2):
            pass_on(g, at(h, du, 0, j), q1_rs.at[g * 32 + n * 8 + four(way, h, j)], near(h, 0, 1 - 2 * way))

    def gather_own(g):
        own_copies[g].wait()
        others(lambda zz: wait(grads[g].at[r * LB + zz // 2, :, lanes_in_block(zz)], gz_rs.at[g * FEAT + zz]))
        for way in range(2):
            for h in range(2):
                for j in (way, 1 - way):
                    pass_on(g, at(h, 0, 0, j), p1_rs.at[8 * g + four(way, h, j)], near(h, 1 - 2 * way, 0))
        for h in range(2):
            for j in range(2):
                second_axis(g, 0, 0, h, j)
                share(g, at(h, 0, 0, j))

    def gather_near(g):
        for turn in range(2):
            for way in range(2):
                j = way if turn == 0 else 1 - way
                du = 2 * way - 1
                for h in range(2):
                    block = at(h, du, 0, j)
                    wait(grads[g].at[block], p1_rs.at[8 * g + four(way, h, j)])
                    if j == way:
                        pass_on(g, block, p2_rs.at[4 * g + 2 * h + way], near(h, 1 - 2 * way, 0))
                    second_axis(g, 1 + way, du, h, j)
                    share(g, block)

    def gather_far(g):
        for h in range(2):
            for j in range(2):
                block = at(h, 2, 0, j)
                wait(grads[g].at[block], p2_rs.at[4 * g + 2 * h + j])
                second_axis(g, 3, 2, h, j)
                share(g, block)

    offs = (0, -1, 1, 2)

    def take(g, n):
        for way in range(2):
            for h in range(2):
                for j in (way, 1 - way):
                    block = at(h, offs[n], 2 * way - 1, j)
                    wait(grads[g].at[block], q1_rs.at[g * 32 + n * 8 + four(way, h, j)])
                    if j == way:
                        pass_on(g, block, q2_rs.at[g * 16 + n * 4 + 2 * h + way], near(h, 0, 1 - 2 * way))
                    share(g, block)

    def take_last(g):
        for n in range(4):
            for h in range(2):
                for j in range(2):
                    block = at(h, offs[n], 2, j)
                    wait(grads[g].at[block], q2_rs.at[g * 16 + n * 4 + 2 * h + j])
                    share(g, block)

    def backward_ready(g):
        wait(grads[g].at[pl.ds(0, 64)], pair_rs.at[g])

    def backward(g, first, last):
        def batch(b):
            left, right = [], []
            for k in range(GROUP):
                p = b * GROUP + k
                grad = grads[g][label_ref[p]]
                tile = lax.rem(doc_ref[p], tile_count)
                left.append(
                    jnp.concatenate(
                        [jnp.where(tile == t, grad, jnp.zeros_like(grad)) for t in range(tile_count)], axis=0
                    )
                )
                right.append(inc_buf[g * PAIRS + p])
            fg_acc[...] += lax.dot_general(
                jnp.concatenate(left, axis=1), jnp.concatenate(right, axis=1),
                (((1,), (1,)), ((), ())), preferred_element_type=f32,
            )

        loop(last, batch, first)

    def backward_done():
        for t in range(tile_count):
            fg_out[:, t * TILE : (t + 1) * TILE] = fg_acc[t * W : (t + 1) * W, :].astype(bf16)

    HALF = W // 2

    def slab(s, cc):
        return pl.ds(pl.multiple_of(s * W + cc * HALF, HALF), HALF)

    def weight_inputs(g):
        lanes = group_lanes(g)
        send(xin.at[:, lanes], x_pair.at[:, lanes], wg_ss.at[0], wgc_rs.at[2 * g], sibling)
        send(gm_buf.at[:, lanes], gm_pair.at[:, lanes], wg_ss.at[0], wgc_rs.at[2 * g + 1], sibling)

    def weight_to_z():
        for g in range(2):
            wait(x_pair.at[:, group_lanes(g)], wgc_rs.at[2 * g])
            wait(gm_pair.at[:, group_lanes(g)], wgc_rs.at[2 * g + 1])

        def term(zz):
            total = 0
            for left, right in ((xin, gm_buf), (x_pair, gm_pair)):
                total = total + lax.dot_general(
                    left[slab(zz, core), :], right[...], (((1,), (1,)), ((), ())), preferred_element_type=f32
                )
            return total

        def one(zz):
            wgz_send[zz] = term(zz).astype(bf16)
            send(wgz_send.at[zz], wgz_recv.at[z], wg_ss.at[1], wgz_rs.at[z], to(zz))

        others(one)
        wg_half[...] = term(z)

    def weight_to_x():
        def one(zz):
            wait(wgz_recv.at[zz], wgz_rs.at[zz])
            wg_half[...] += wgz_recv[zz].astype(f32)

        others(one)
        for t in range(36):
            a, b = t // 6, t % 6
            wx_send[t // 9, t % 9] = wg_half[8 * a : 8 * a + 8, 128 * b : 128 * b + 128]
        for d in range(1, SIDE):
            xx = around(x, d)
            send(wx_send.at[xx], wx_recv.at[x], wg_ss.at[2], wx_rs.at[x], near(0, d, 0))

    def weight_to_y():
        total = wx_send[x]
        for d in range(1, SIDE):
            xx = around(x, d)
            wait(wx_recv.at[xx], wx_rs.at[xx])
            total = total + wx_recv[xx]
        wy_send[...] = total
        wy_recv[y] = total
        for d in range(1, SIDE):
            send(wy_send, wy_recv.at[y], wg_ss.at[3], wy_rs.at[y], near(1, d, 0))

    def weight_back_x():
        for d in range(1, SIDE):
            yy = around(y, d)
            wait(wy_recv.at[yy], wy_rs.at[yy])
        total = (wy_recv[0] + wy_recv[1]) + (wy_recv[2] + wy_recv[3])
        wf_send[...] = total
        wf_recv[x] = total
        for d in range(1, SIDE):
            send(wf_send, wf_recv.at[x], wg_ss.at[4], wf_rs.at[x], near(0, d, 0))

    mine = pl.ds(pl.multiple_of(core * HALF, HALF), HALF)
    other = pl.ds(pl.multiple_of((1 - core) * HALF, HALF), HALF)
    own_wg = pltpu.make_async_copy(wg_half, wg_out.at[mine, :], local_sem.at[4])

    def weight_done():
        for d in range(1, SIDE):
            xx = around(x, d)
            wait(wf_recv.at[xx], wf_rs.at[xx])
        for t in range(36):
            a, b = t // 6, t % 6
            wg_half[8 * a : 8 * a + 8, 128 * b : 128 * b + 128] = wf_recv[t // 9, t % 9]
        send(wg_half, wg_out.at[mine, :], wg_ss.at[5], wl_rs, sibling)
        own_wg.start()

    weight_start()
    spread_cotangent()
    messages(0)
    wait(tab_in, tab_sems.at[2])
    sib_tab = pltpu.make_async_copy(tab_in, tab_sib, tab_sems.at[3])
    sib_tab.start()
    own_tab.wait()
    sib_tab.wait()
    pair_messages_in(0)
    far(0)
    close(0, False)
    messages(1)
    close(0, True)
    pair_messages_in(1)
    far(1)
    second_axis_sums(0)
    close(1, False)
    finish_sums(0)
    close(1, True)
    weight_share()
    mix(0)
    second_axis_sums(1)
    gather_own(0)
    finish_sums(1)
    give_act(0)
    gather_near(0)
    weight_inputs(0)
    gather_far(0)
    mix(1)
    weight_inputs(1)
    take(0, 0)
    take(0, 1)
    take(0, 2)
    weight_to_z()
    take(0, 3)
    gather_own(1)
    give_act(1)
    fg_acc[...] = jnp.zeros_like(fg_acc)
    take_last(0)
    gather_near(1)
    gather_far(1)
    backward_ready(0)
    backward(0, 0, 3)
    take(1, 0)
    backward(0, 3, 6)
    take(1, 1)
    take(1, 2)
    weight_to_x()
    take(1, 3)
    weight_to_y()
    take_last(1)
    weight_back_x()
    backward_ready(1)
    backward(1, 0, 3)
    weight_done()
    backward(1, 3, BATCHES)
    backward_done()

    own_wg.wait()
    wait(wg_out.at[other, :], wl_rs)
    for g in range(2):
        own_acts[g].wait()
        others(lambda zz: wait(act_out.at[:, lanes_in_all(zz, g)], act_rs.at[g * FEAT + zz]))
    for g in range(2):
        wait(msg[g].at[pl.ds(0, PAIRS)], sib_ss.at[g])
        wait(grads[g].at[pl.ds(0, 124)], ag_ss.at[g])
    wait(tab_out, tab_sems.at[1])
    wait(s1_send, s1_ss)
    wait(s2_send, s2_ss)
    wait(t1_send, t_ss.at[0])
    wait(t2_send, t_ss.at[1])
    seven = pl.ds(0, (FEAT - 1) * W)
    for k in (0, 5):
        wait(wfull.at[seven, half_cols], z_ss.at[k])
    for k in range(1, 5):
        wait(cot_in.at[seven, :], z_ss.at[k])
    wait(wfull.at[:, pl.ds(0, 2 * CHUNK)], wg_ss.at[0])
    wait(wgz_send.at[pl.ds(0, FEAT - 1)], wg_ss.at[1])
    for k in (2, 3, 4):
        wait(wx_send.at[pl.ds(0, SIDE - 1)], wg_ss.at[k])
    wait(wg_half, wg_ss.at[5])


def exchange(doc, label, feat, inc, weight, cot):
    dma = pltpu.SemaphoreType.DMA
    block = (W, CHUNK)
    vmem = pltpu.VMEM
    smem_spec = pl.BlockSpec(memory_space=pltpu.SMEM)
    any_spec = pl.BlockSpec(memory_space=pl.ANY)
    vmem_spec = pl.BlockSpec(memory_space=pltpu.VMEM)
    table = ((8, BLOCKS), jnp.int32)
    return pl.pallas_call(
        exchange_kernel,
        in_specs=[smem_spec, smem_spec, vmem_spec, any_spec, vmem_spec, vmem_spec],
        out_specs=[any_spec, any_spec, vmem_spec],
        out_shape=[
            jax.ShapeDtypeStruct(cot.shape, bf16),
            jax.ShapeDtypeStruct((W, D), f32),
            jax.ShapeDtypeStruct(feat.shape, bf16),
        ],
        scratch_shapes=[
            vmem((BLOCKS, *block), bf16), vmem((BLOCKS, *block), bf16),
            vmem((feat.shape[1] // TILE * W, TILE), f32),
            vmem((feat.shape[1] // TILE, W, TILE), bf16),
            vmem((2 * PAIRS, TILE, CHUNK), bf16), vmem((NONE + 1, *block), bf16), vmem((NONE + 1, *block), bf16),
            vmem(*table), vmem(*table), vmem(*table), pltpu.SMEM(*table), pltpu.SMEM(*table),
            vmem((32, *block), bf16), vmem((32, *block), bf16),
            vmem((64, *block), bf16), vmem((64, *block), bf16),
            vmem((8, *block), bf16), vmem((8, *block), bf16),
            vmem((16, *block), bf16), vmem((16, *block), bf16),
            vmem((2 * LB, *block), bf16),
            vmem((D, CHUNK), bf16), vmem((D, D), bf16), vmem((D, CHUNK), bf16),
            vmem((D, CHUNK), bf16), vmem((D, CHUNK), bf16), vmem((D, CHUNK), bf16),
            vmem((D, CHUNK), bf16), vmem((D, CHUNK), bf16),
            vmem((FEAT, W // 2, D), bf16), vmem((FEAT, W // 2, D), bf16),
            vmem((SIDE, 9, 8, 128), f32), vmem((SIDE, 9, 8, 128), f32),
            vmem((9, 8, 128), f32), vmem((SIDE, 9, 8, 128), f32),
            vmem((9, 8, 128), f32), vmem((SIDE, 9, 8, 128), f32),
            vmem((W // 2, D), f32),
            dma((2 * BATCHES,)), dma((4,)), dma((2,)), dma((2 * BATCHES,)),
            dma, dma((32,)), dma, dma((64,)), dma((2,)), dma((8,)), dma((16,)),
            dma((6,)), dma((2 * FEAT,)), dma((2 * FEAT,)), dma((2 * FEAT,)), dma((2 * FEAT,)), dma((2 * FEAT,)), dma((5,)),
            dma((2,)), dma((16,)), dma((8,)), dma((64,)), dma((32,)), dma((2,)),
            dma((6,)), dma((4,)), dma((FEAT,)), dma((SIDE,)), dma((SIDE,)), dma((SIDE,)), dma,
        ],
        compiler_params=pltpu.CompilerParams(
            collective_id=0, has_side_effects=True, vmem_limit_bytes=VMEM_LIMIT
        ),
    )(doc, label, feat, inc, weight, cot)


def local(features, pair_doc, pair_label, incidence, weight, cotangent):
    act, weight_grad, feature_grad = exchange(
        pair_doc, pair_label, features.T, incidence, weight, cotangent.T
    )
    return act.T, weight_grad, feature_grad.T


def solution(mesh):
    return jax.shard_map(
        local,
        mesh=mesh,
        in_specs=(
            P("rows", "feat"),
            P("rows"),
            P("rows"),
            P("rows", None, None),
            P("feat", None),
            P("rows", "feat"),
        ),
        out_specs=(P("rows", "feat"), P("feat", None), P("rows", "feat")),
        check_vma=False,
    )
```

```python
import functools

import jax
import jax.numpy as jnp
from jax import lax
from jax.experimental import pallas as pl
from jax.experimental.pallas import tpu as pltpu
from jax.sharding import PartitionSpec as P

MESH = pl.DeviceIdType.MESH
message_scale = 0.0625

SIDE = 4
FEAT = 8
LB = 4
CAP = 3
TILE = 512
PAIRS = 24
W = 96
D = 768
GROUP = 4
BLOCKS = 128
CHUNK = 256
PART = 128
BATCHES = PAIRS // GROUP
NONE = 2 * PAIRS
VMEM_LIMIT = 60 * 1024 * 1024

f32, bf16 = jnp.float32, jnp.bfloat16


def wait(ref, sem):
    pltpu.make_async_copy(ref, ref, sem).wait()


def offset(i):
    return 2 - i + 3 * (i // 2) - 2 * (i // 3)


def exchange_kernel(
    doc_ref, label_ref, feat, inc, weight, cot,
    act_out, wg_out, fg_out,
    grads_a, grads_b, fg_acc,
    tiles, inc_buf, msg_a, msg_b, tab, tab_out, tab_in, tab_own, tab_sib,
    s1_send, s1_recv, s2_send, s2_recv, t1_send, t1_recv, t2_send, t2_recv,
    summed, xin, wfull, cot_in, act_buf, gm_buf, gmt_buf,
    x_pair, gm_pair, wgz_send, wgz_recv, wx_send, wx_recv, wy_send, wy_recv, wf_send, wf_recv, wg_half,
    inc_sem, tab_sems, sib_ss, sib_rs, s1_ss, s1_rs, s2_ss, s2_rs, t_ss, t1_rs, t2_rs,
    z_ss, x_rs, w_rs, cot_rs, act_rs, gz_rs, local_sem,
    ag_ss, p1_rs, p2_rs, q1_rs, q2_rs, pair_rs,
    wg_ss, wgc_rs, wgz_rs, wx_rs, wy_rs, wf_rs, wl_rs,
):
    r, z = lax.axis_index("rows"), lax.axis_index("feat")
    core, x, y = lax.rem(r, 2), lax.rem(r // 2, SIDE), r // (2 * SIDE)

    def around(value, step):
        return lax.rem(value + step + 2 * SIDE, SIDE)

    def row_of(yy, xx, cc):
        return (yy * SIDE + xx) * 2 + cc

    place = ((x, y), (y, x))
    msg = (msg_a, msg_b)
    grads = (grads_a, grads_b)

    def owner(h, u, v, cc):
        return row_of(v, u, cc) if h == 0 else row_of(u, v, cc)

    def near(h, du, dv):
        u, v = place[h]
        return {"rows": owner(h, around(u, du), around(v, dv), core), "feat": z}

    sibling = {"rows": row_of(y, x, 1 - core), "feat": z}

    def along_z(d):
        return lax.rem(z + d, FEAT)

    def send(src, dst, ss, rs, target):
        pltpu.make_async_remote_copy(
            src_ref=src, dst_ref=dst, send_sem=ss, recv_sem=rs, device_id=target, device_id_type=MESH
        ).start()

    def loop(n, body, start=0):
        lax.fori_loop(start, n, lambda i, c: (body(i), c)[1], 0)

    def others(body):
        loop(FEAT, lambda d: body(along_z(d)), 1)

    barrier = pltpu.get_barrier_semaphore()
    partners = [sibling]
    for d in range(1, SIDE):
        partners += [near(0, d, 0), near(1, d, 0)]
    for d in range(1, FEAT):
        partners.append({"rows": r, "feat": along_z(d)})
    for target in partners:
        pl.semaphore_signal(barrier, inc=1, device_id=target, device_id_type=MESH)

    def inc_copy(g, b):
        return pltpu.make_async_copy(
            inc.at[pl.ds(b * GROUP, GROUP), :, pl.ds(g * CHUNK, CHUNK)],
            inc_buf.at[pl.ds((g * BATCHES + b) * GROUP, GROUP)],
            inc_sem.at[g * BATCHES + b],
        )

    for g in range(2):
        for b in range(BATCHES):
            inc_copy(g, b).start()

    lane = lax.broadcasted_iota(jnp.int32, (1, BLOCKS), 1)
    count = jnp.zeros((1, BLOCKS), jnp.int32)
    spots = [jnp.full((1, BLOCKS), NONE, jnp.int32) for _ in range(CAP)]
    for p in range(PAIRS):
        hit = lane == label_ref[p]
        spots = [jnp.where(hit & (count == k), p, spots[k]) for k in range(CAP)]
        count = count + jnp.where(hit, 1, 0)
    tab[...] = jnp.full(tab.shape, NONE, jnp.int32)
    tab_out[...] = jnp.full(tab.shape, NONE, jnp.int32)
    for k in range(CAP):
        tab[k : k + 1, :] = spots[k]
        tab_out[k : k + 1, :] = jnp.where(spots[k] < NONE, spots[k] + PAIRS, NONE)
    own_tab = pltpu.make_async_copy(tab, tab_own, tab_sems.at[0])
    own_tab.start()
    for t in range(feat.shape[1] // TILE):
        tiles[t] = feat[:, t * TILE : (t + 1) * TILE]
    for g in range(2):
        msg[g][NONE] = jnp.zeros((W, CHUNK), bf16)

    pl.semaphore_wait(barrier, len(partners))
    send(tab_out, tab_in, tab_sems.at[1], tab_sems.at[2], sibling)

    tile_count = feat.shape[1] // TILE

    def messages(g):
        def batch(b):
            inc_copy(g, b).wait()
            for k in range(GROUP):
                p = b * GROUP + k
                product = jnp.dot(
                    tiles[lax.rem(doc_ref[p], tile_count)], inc_buf[g * PAIRS + p], preferred_element_type=f32
                )
                msg[g][p] = (message_scale * product).astype(bf16)
            send(
                msg[g].at[pl.ds(b * GROUP, GROUP)], msg[g].at[pl.ds(PAIRS + b * GROUP, GROUP)],
                sib_ss.at[g], sib_rs.at[g * BATCHES + b], sibling,
            )

        loop(BATCHES, batch)

    def pair_messages_in(g):
        def one(b):
            wait(msg[g].at[pl.ds(PAIRS + b * GROUP, GROUP)], sib_rs.at[g * BATCHES + b])

        loop(BATCHES, one)

    def block_id(h, u, v, j, cc):
        return owner(h, u, v, cc) * LB + 2 * h + j

    def part(g, h, du, dv, j):
        u, v = place[h]
        block = block_id(h, around(u, du), around(v, dv), j, core)
        total = msg[g][tab_own[0, block]].astype(f32)
        for k in range(1, CAP):
            total = total + msg[g][tab_own[k, block]].astype(f32)
        for k in range(CAP):
            total = total + msg[g][tab_sib[k, block]].astype(f32)
        return total

    def slot(g, a, i, h, j):
        return (((a * 2 + g) * SIDE + i) * 2 + h) * 2 + j

    def far(g):
        def one(i):
            for h in range(2):
                for j in range(2):
                    k = slot(g, 0, i, h, j)
                    s1_send[k] = part(g, h, 2, offset(i), j).astype(bf16)
                    send(s1_send.at[k], s1_recv.at[k], s1_ss, s1_rs.at[k], near(h, 1 - 2 * j, 0))

        loop(SIDE, one)

    def close(g, passed):
        def one(i):
            for h in range(2):
                for way in range(2):
                    du = 1 - 2 * way
                    j = way if passed else 1 - way
                    k = slot(g, way, i, h, j)
                    total = part(g, h, du, offset(i), j)
                    if passed:
                        q = slot(g, 0, i, h, j)
                        wait(s1_recv.at[q], s1_rs.at[q])
                        total = total + s1_recv[q].astype(f32)
                    s2_send[k] = total.astype(bf16)
                    send(s2_send.at[k], s2_recv.at[k], s2_ss, s2_rs.at[k], near(h, du, 0))

        loop(SIDE, one)

    def column(g, i, h, j):
        total = part(g, h, 0, offset(i), j)
        for way in (1 - j, j):
            k = slot(g, way, i, h, j)
            wait(s2_recv.at[k], s2_rs.at[k])
            total = total + s2_recv[k].astype(f32)
        return total

    def four(way, h, j):
        return (way * 2 + h) * 2 + j

    def second_axis_sums(g):
        for h in range(2):
            for j in range(2):
                k = 4 * g + 2 * h + j
                t1_send[k] = column(g, 0, h, j).astype(bf16)
                send(t1_send.at[k], t1_recv.at[k], t_ss.at[0], t1_rs.at[k], near(h, 0, 1 - 2 * j))
        for passed in (False, True):
            for way in range(2):
                for h in range(2):
                    j = way if passed else 1 - way
                    k = 8 * g + four(way, h, j)
                    total = column(g, 1 + way, h, j)
                    if passed:
                        q = 4 * g + 2 * h + j
                        wait(t1_recv.at[q], t1_rs.at[q])
                        total = total + t1_recv[q].astype(f32)
                    t2_send[k] = total.astype(bf16)
                    send(t2_send.at[k], t2_recv.at[k], t_ss.at[1], t2_rs.at[k], near(h, 0, 1 - 2 * way))

    own_rows = pl.ds(pl.multiple_of(z * W, W), W)

    def rows_at(zz):
        return pl.ds(pl.multiple_of(zz * W, W), W)

    def lanes_in_block(zz, base=0):
        return pl.ds(pl.multiple_of(base + lax.rem(zz, 2) * PART, PART), PART)

    def lanes_in_all(zz, g):
        return pl.ds(pl.multiple_of((zz // 2) * TILE + g * CHUNK + lax.rem(zz, 2) * PART, PART), PART)

    def group_lanes(g):
        return pl.ds(g * PART, PART)

    def to(zz):
        return {"rows": r, "feat": zz}

    def finish_sums(g):
        for h in range(2):
            for j in range(2):
                total = column(g, 3, h, j)
                for way in (1 - j, j):
                    k = 8 * g + four(way, h, j)
                    wait(t2_recv.at[k], t2_rs.at[k])
                    total = total + t2_recv[k].astype(f32)
                summed[g * LB + 2 * h + j] = total.astype(bf16)

        def one(zz):
            send(summed.at[g * LB + zz // 2, :, lanes_in_block(zz)], xin.at[own_rows, group_lanes(g)],
                 z_ss.at[2], x_rs.at[g * FEAT + z], to(zz))

        others(one)
        xin[own_rows, group_lanes(g)] = summed[g * LB + z // 2, :, lanes_in_block(z)]

    half_cols = pl.ds(pl.multiple_of(core * (D // 2), D // 2), D // 2)
    other_cols = pl.ds(pl.multiple_of((1 - core) * (D // 2), D // 2), D // 2)

    def weight_start():
        others(lambda zz: send(weight.at[:, half_cols], wfull.at[own_rows, half_cols], z_ss.at[0], w_rs.at[z], to(zz)))
        wfull[own_rows, :] = weight[...]

    def weight_share():
        def one(zz):
            half = wfull.at[rows_at(zz), half_cols]
            wait(half, w_rs.at[zz])
            send(half, half, z_ss.at[5], w_rs.at[FEAT + zz], sibling)

        others(one)

    def spread_cotangent():
        def one(zz):
            for g in range(2):
                send(cot.at[:, lanes_in_all(zz, g)], cot_in.at[own_rows, group_lanes(g)],
                     z_ss.at[1], cot_rs.at[g * FEAT + z], to(zz))

        others(one)
        for g in range(2):
            cot_in[own_rows, group_lanes(g)] = cot[:, lanes_in_all(z, g)]

    own_copies = []

    def mix(g):
        if g == 0:
            others(lambda zz: wait(wfull.at[rows_at(zz), other_cols], w_rs.at[FEAT + zz]))
            for gg in range(2):
                others(lambda zz: wait(cot_in.at[rows_at(zz), group_lanes(gg)], cot_rs.at[gg * FEAT + zz]))
        others(lambda zz: wait(xin.at[rows_at(zz), group_lanes(g)], x_rs.at[g * FEAT + zz]))

        def forth(o):
            rows = pl.ds(pl.multiple_of(o * CHUNK, CHUNK), CHUNK)
            mixed = lax.dot_general(
                wfull[:, rows], xin[:, group_lanes(g)], (((0,), (0,)), ((), ())), preferred_element_type=f32
            )
            gate = jax.nn.sigmoid(mixed)
            act_buf[rows, group_lanes(g)] = (mixed * gate).astype(bf16)
            slope = gate * (1.0 + mixed * (1.0 - gate))
            gm_buf[rows, group_lanes(g)] = (cot_in[rows, group_lanes(g)].astype(f32) * slope).astype(bf16)

        loop(D // CHUNK, forth)

        def back(o):
            rows = pl.ds(pl.multiple_of(o * CHUNK, CHUNK), CHUNK)
            gmt_buf[rows, group_lanes(g)] = jnp.dot(
                wfull[rows, :], gm_buf[:, group_lanes(g)], preferred_element_type=f32
            ).astype(bf16)

        loop(D // CHUNK, back)
        mine = grads[g].at[r * LB + z // 2, :, lanes_in_block(z)]
        others(lambda zz: send(gmt_buf.at[rows_at(zz), group_lanes(g)], mine, z_ss.at[3], gz_rs.at[g * FEAT + z], to(zz)))
        own = pltpu.make_async_copy(gmt_buf.at[own_rows, group_lanes(g)], mine, local_sem.at[g])
        own.start()
        own_copies.append(own)

    own_acts = []

    def give_act(g):
        there = act_out.at[:, lanes_in_all(z, g)]
        others(lambda zz: send(act_buf.at[rows_at(zz), group_lanes(g)], there, z_ss.at[4], act_rs.at[g * FEAT + z], to(zz)))
        own_act = pltpu.make_async_copy(act_buf.at[own_rows, group_lanes(g)], there, local_sem.at[2 + g])
        own_act.start()
        own_acts.append(own_act)

    def share(g, block):
        send(grads[g].at[block], grads[g].at[block], ag_ss.at[g], pair_rs.at[g], sibling)

    def pass_on(g, block, rs, target):
        send(grads[g].at[block], grads[g].at[block], ag_ss.at[g], rs, target)

    def at(h, du, dv, j):
        u, v = place[h]
        return block_id(h, around(u, du), around(v, dv), j, core)

    def second_axis(g, n, du, h, j):
        for way in range(2):
            pass_on(g, at(h, du, 0, j), q1_rs.at[g * 32 + n * 8 + four(way, h, j)], near(h, 0, 1 - 2 * way))

    def gather_own(g):
        own_copies[g].wait()
        others(lambda zz: wait(grads[g].at[r * LB + zz // 2, :, lanes_in_block(zz)], gz_rs.at[g * FEAT + zz]))
        for way in range(2):
            for h in range(2):
                for j in (way, 1 - way):
                    pass_on(g, at(h, 0, 0, j), p1_rs.at[8 * g + four(way, h, j)], near(h, 1 - 2 * way, 0))
        for h in range(2):
            for j in range(2):
                second_axis(g, 0, 0, h, j)
                share(g, at(h, 0, 0, j))

    def gather_near(g):
        for turn in range(2):
            for way in range(2):
                j = way if turn == 0 else 1 - way
                du = 2 * way - 1
                for h in range(2):
                    block = at(h, du, 0, j)
                    wait(grads[g].at[block], p1_rs.at[8 * g + four(way, h, j)])
                    if j == way:
                        pass_on(g, block, p2_rs.at[4 * g + 2 * h + way], near(h, 1 - 2 * way, 0))
                    second_axis(g, 1 + way, du, h, j)
                    share(g, block)

    def gather_far(g):
        for h in range(2):
            for j in range(2):
                block = at(h, 2, 0, j)
                wait(grads[g].at[block], p2_rs.at[4 * g + 2 * h + j])
                second_axis(g, 3, 2, h, j)
                share(g, block)

    offs = (0, -1, 1, 2)

    def take(g, n):
        for way in range(2):
            for h in range(2):
                for j in (way, 1 - way):
                    block = at(h, offs[n], 2 * way - 1, j)
                    wait(grads[g].at[block], q1_rs.at[g * 32 + n * 8 + four(way, h, j)])
                    if j == way:
                        pass_on(g, block, q2_rs.at[g * 16 + n * 4 + 2 * h + way], near(h, 0, 1 - 2 * way))
                    share(g, block)

    def take_last(g):
        for n in range(4):
            for h in range(2):
                for j in range(2):
                    block = at(h, offs[n], 2, j)
                    wait(grads[g].at[block], q2_rs.at[g * 16 + n * 4 + 2 * h + j])
                    share(g, block)

    def backward_ready(g):
        wait(grads[g].at[pl.ds(0, 64)], pair_rs.at[g])

    def backward(g, first, last):
        def batch(b):
            left, right = [], []
            for k in range(GROUP):
                p = b * GROUP + k
                grad = grads[g][label_ref[p]]
                tile = lax.rem(doc_ref[p], tile_count)
                left.append(
                    jnp.concatenate(
                        [jnp.where(tile == t, grad, jnp.zeros_like(grad)) for t in range(tile_count)], axis=0
                    )
                )
                right.append(inc_buf[g * PAIRS + p])
            fg_acc[...] += lax.dot_general(
                jnp.concatenate(left, axis=1), jnp.concatenate(right, axis=1),
                (((1,), (1,)), ((), ())), preferred_element_type=f32,
            )

        loop(last, batch, first)

    def backward_done():
        for t in range(tile_count):
            fg_out[:, t * TILE : (t + 1) * TILE] = fg_acc[t * W : (t + 1) * W, :].astype(bf16)

    HALF = W // 2

    def slab(s, cc):
        return pl.ds(pl.multiple_of(s * W + cc * HALF, HALF), HALF)

    def weight_inputs(g):
        lanes = group_lanes(g)
        send(xin.at[:, lanes], x_pair.at[:, lanes], wg_ss.at[0], wgc_rs.at[2 * g], sibling)
        send(gm_buf.at[:, lanes], gm_pair.at[:, lanes], wg_ss.at[0], wgc_rs.at[2 * g + 1], sibling)

    def weight_to_z():
        for g in range(2):
            wait(x_pair.at[:, group_lanes(g)], wgc_rs.at[2 * g])
            wait(gm_pair.at[:, group_lanes(g)], wgc_rs.at[2 * g + 1])

        def term(zz):
            total = 0
            for left, right in ((xin, gm_buf), (x_pair, gm_pair)):
                total = total + lax.dot_general(
                    left[slab(zz, core), :], right[...], (((1,), (1,)), ((), ())), preferred_element_type=f32
                )
            return total

        def one(zz):
            wgz_send[zz] = term(zz).astype(bf16)
            send(wgz_send.at[zz], wgz_recv.at[z], wg_ss.at[1], wgz_rs.at[z], to(zz))

        others(one)
        wg_half[...] = term(z)

    def weight_to_x():
        def one(zz):
            wait(wgz_recv.at[zz], wgz_rs.at[zz])
            wg_half[...] += wgz_recv[zz].astype(f32)

        others(one)
        for t in range(36):
            a, b = t // 6, t % 6
            wx_send[t // 9, t % 9] = wg_half[8 * a : 8 * a + 8, 128 * b : 128 * b + 128]
        for d in range(1, SIDE):
            xx = around(x, d)
            send(wx_send.at[xx], wx_recv.at[x], wg_ss.at[2], wx_rs.at[x], near(0, d, 0))

    def weight_to_y():
        total = wx_send[x]
        for d in range(1, SIDE):
            xx = around(x, d)
            wait(wx_recv.at[xx], wx_rs.at[xx])
            total = total + wx_recv[xx]
        wy_send[...] = total
        wy_recv[y] = total
        for d in range(1, SIDE):
            send(wy_send, wy_recv.at[y], wg_ss.at[3], wy_rs.at[y], near(1, d, 0))

    def weight_back_x():
        for d in range(1, SIDE):
            yy = around(y, d)
            wait(wy_recv.at[yy], wy_rs.at[yy])
        total = (wy_recv[0] + wy_recv[1]) + (wy_recv[2] + wy_recv[3])
        wf_send[...] = total
        wf_recv[x] = total
        for d in range(1, SIDE):
            send(wf_send, wf_recv.at[x], wg_ss.at[4], wf_rs.at[x], near(0, d, 0))

    mine = pl.ds(pl.multiple_of(core * HALF, HALF), HALF)
    other = pl.ds(pl.multiple_of((1 - core) * HALF, HALF), HALF)
    own_wg = pltpu.make_async_copy(wg_half, wg_out.at[mine, :], local_sem.at[4])

    def weight_done():
        for d in range(1, SIDE):
            xx = around(x, d)
            wait(wf_recv.at[xx], wf_rs.at[xx])
        for t in range(36):
            a, b = t // 6, t % 6
            wg_half[8 * a : 8 * a + 8, 128 * b : 128 * b + 128] = wf_recv[t // 9, t % 9]
        send(wg_half, wg_out.at[mine, :], wg_ss.at[5], wl_rs, sibling)
        own_wg.start()

    weight_start()
    spread_cotangent()
    messages(0)
    wait(tab_in, tab_sems.at[2])
    sib_tab = pltpu.make_async_copy(tab_in, tab_sib, tab_sems.at[3])
    sib_tab.start()
    own_tab.wait()
    sib_tab.wait()
    pair_messages_in(0)
    far(0)
    close(0, False)
    messages(1)
    close(0, True)
    second_axis_sums(0)
    pair_messages_in(1)
    far(1)
    close(1, False)
    finish_sums(0)
    close(1, True)
    weight_share()
    mix(0)
    second_axis_sums(1)
    gather_own(0)
    finish_sums(1)
    give_act(0)
    gather_near(0)
    weight_inputs(0)
    gather_far(0)
    mix(1)
    weight_inputs(1)
    take(0, 0)
    take(0, 1)
    take(0, 2)
    weight_to_z()
    take(0, 3)
    gather_own(1)
    give_act(1)
    fg_acc[...] = jnp.zeros_like(fg_acc)
    take_last(0)
    gather_near(1)
    gather_far(1)
    backward_ready(0)
    backward(0, 0, 3)
    take(1, 0)
    backward(0, 3, 6)
    take(1, 1)
    take(1, 2)
    weight_to_x()
    take(1, 3)
    weight_to_y()
    take_last(1)
    weight_back_x()
    backward_ready(1)
    backward(1, 0, 3)
    weight_done()
    backward(1, 3, BATCHES)
    backward_done()

    own_wg.wait()
    wait(wg_out.at[other, :], wl_rs)
    for g in range(2):
        own_acts[g].wait()
        others(lambda zz: wait(act_out.at[:, lanes_in_all(zz, g)], act_rs.at[g * FEAT + zz]))
    for g in range(2):
        wait(msg[g].at[pl.ds(0, PAIRS)], sib_ss.at[g])
        wait(grads[g].at[pl.ds(0, 124)], ag_ss.at[g])
    wait(tab_out, tab_sems.at[1])
    wait(s1_send, s1_ss)
    wait(s2_send, s2_ss)
    wait(t1_send, t_ss.at[0])
    wait(t2_send, t_ss.at[1])
    seven = pl.ds(0, (FEAT - 1) * W)
    for k in (0, 5):
        wait(wfull.at[seven, half_cols], z_ss.at[k])
    for k in range(1, 5):
        wait(cot_in.at[seven, :], z_ss.at[k])
    wait(wfull.at[:, pl.ds(0, 2 * CHUNK)], wg_ss.at[0])
    wait(wgz_send.at[pl.ds(0, FEAT - 1)], wg_ss.at[1])
    for k in (2, 3, 4):
        wait(wx_send.at[pl.ds(0, SIDE - 1)], wg_ss.at[k])
    wait(wg_half, wg_ss.at[5])


def exchange(doc, label, feat, inc, weight, cot):
    dma = pltpu.SemaphoreType.DMA
    block = (W, CHUNK)
    vmem = pltpu.VMEM
    smem_spec = pl.BlockSpec(memory_space=pltpu.SMEM)
    any_spec = pl.BlockSpec(memory_space=pl.ANY)
    vmem_spec = pl.BlockSpec(memory_space=pltpu.VMEM)
    table = ((8, BLOCKS), jnp.int32)
    return pl.pallas_call(
        exchange_kernel,
        in_specs=[smem_spec, smem_spec, vmem_spec, any_spec, vmem_spec, vmem_spec],
        out_specs=[any_spec, any_spec, vmem_spec],
        out_shape=[
            jax.ShapeDtypeStruct(cot.shape, bf16),
            jax.ShapeDtypeStruct((W, D), f32),
            jax.ShapeDtypeStruct(feat.shape, bf16),
        ],
        scratch_shapes=[
            vmem((BLOCKS, *block), bf16), vmem((BLOCKS, *block), bf16),
            vmem((feat.shape[1] // TILE * W, TILE), f32),
            vmem((feat.shape[1] // TILE, W, TILE), bf16),
            vmem((2 * PAIRS, TILE, CHUNK), bf16), vmem((NONE + 1, *block), bf16), vmem((NONE + 1, *block), bf16),
            vmem(*table), vmem(*table), vmem(*table), pltpu.SMEM(*table), pltpu.SMEM(*table),
            vmem((32, *block), bf16), vmem((32, *block), bf16),
            vmem((64, *block), bf16), vmem((64, *block), bf16),
            vmem((8, *block), bf16), vmem((8, *block), bf16),
            vmem((16, *block), bf16), vmem((16, *block), bf16),
            vmem((2 * LB, *block), bf16),
            vmem((D, CHUNK), bf16), vmem((D, D), bf16), vmem((D, CHUNK), bf16),
            vmem((D, CHUNK), bf16), vmem((D, CHUNK), bf16), vmem((D, CHUNK), bf16),
            vmem((D, CHUNK), bf16), vmem((D, CHUNK), bf16),
            vmem((FEAT, W // 2, D), bf16), vmem((FEAT, W // 2, D), bf16),
            vmem((SIDE, 9, 8, 128), f32), vmem((SIDE, 9, 8, 128), f32),
            vmem((9, 8, 128), f32), vmem((SIDE, 9, 8, 128), f32),
            vmem((9, 8, 128), f32), vmem((SIDE, 9, 8, 128), f32),
            vmem((W // 2, D), f32),
            dma((2 * BATCHES,)), dma((4,)), dma((2,)), dma((2 * BATCHES,)),
            dma, dma((32,)), dma, dma((64,)), dma((2,)), dma((8,)), dma((16,)),
            dma((6,)), dma((2 * FEAT,)), dma((2 * FEAT,)), dma((2 * FEAT,)), dma((2 * FEAT,)), dma((2 * FEAT,)), dma((5,)),
            dma((2,)), dma((16,)), dma((8,)), dma((64,)), dma((32,)), dma((2,)),
            dma((6,)), dma((4,)), dma((FEAT,)), dma((SIDE,)), dma((SIDE,)), dma((SIDE,)), dma,
        ],
        compiler_params=pltpu.CompilerParams(
            collective_id=0, has_side_effects=True, vmem_limit_bytes=VMEM_LIMIT
        ),
    )(doc, label, feat, inc, weight, cot)


def results_kernel(*refs):
    half = len(refs) // 2
    ins, outs, sems = refs[:half], refs[half : 2 * half], refs[-1]
    copies = [pltpu.make_async_copy(i, o, sems.at[k]) for k, (i, o) in enumerate(zip(ins, outs))]
    for copy in copies:
        copy.start()
    for copy in copies:
        copy.wait()


def results(*arrays):
    return pl.pallas_call(
        results_kernel,
        in_specs=[pl.BlockSpec(memory_space=pl.ANY)] * len(arrays),
        out_specs=[pl.BlockSpec(memory_space=pltpu.VMEM)] * len(arrays),
        out_shape=[jax.ShapeDtypeStruct(a.shape, a.dtype) for a in arrays],
        scratch_shapes=[pltpu.SemaphoreType.DMA((len(arrays),))],
    )(*arrays)


def local(features, pair_doc, pair_label, incidence, weight, cotangent):
    act, weight_grad, feature_grad = results(
        *exchange(pair_doc, pair_label, features.T, incidence, weight, cotangent.T)
    )
    return act.T, weight_grad, feature_grad.T


def solution(mesh):
    return jax.shard_map(
        local,
        mesh=mesh,
        in_specs=(
            P("rows", "feat"),
            P("rows"),
            P("rows"),
            P("rows", None, None),
            P("feat", None),
            P("rows", "feat"),
        ),
        out_specs=(P("rows", "feat"), P("feat", None), P("rows", "feat")),
        check_vma=False,
    )
```

```python
import functools

import jax
import jax.numpy as jnp
from jax import lax
from jax.experimental import pallas as pl
from jax.experimental.pallas import tpu as pltpu
from jax.sharding import PartitionSpec as P

MESH = pl.DeviceIdType.MESH
message_scale = 0.0625

SIDE = 4
FEAT = 8
LB = 4
CAP = 3
TILE = 512
PAIRS = 24
W = 96
D = 768
GROUP = 4
BLOCKS = 128
CHUNK = 256
PART = 128
BATCHES = PAIRS // GROUP
NONE = 2 * PAIRS
VMEM_LIMIT = 60 * 1024 * 1024

f32, bf16 = jnp.float32, jnp.bfloat16


def wait(ref, sem):
    pltpu.make_async_copy(ref, ref, sem).wait()


def offset(i):
    return 2 - i + 3 * (i // 2) - 2 * (i // 3)


def exchange_kernel(
    doc_ref, label_ref, feat, inc, weight, cot,
    act_out, wg_out, fg_out,
    grads_a, grads_b, fg_acc,
    tiles, inc_buf, msg_a, msg_b, tab, tab_out, tab_in, tab_own, tab_sib,
    s1_send, s1_recv, s2_send, s2_recv, t1_send, t1_recv, t2_send, t2_recv,
    summed, xin, wfull, cot_in, act_buf, gm_buf, gmt_buf,
    wflip, x_pair, gm_pair, wgz_send, wgz_recv, wx_send, wx_recv, wy_send, wy_recv, wf_send, wf_recv, wg_half,
    inc_sem, tab_sems, sib_ss, sib_rs, s1_ss, s1_rs, s2_ss, s2_rs, t_ss, t1_rs, t2_rs,
    z_ss, x_rs, w_rs, cot_rs, act_rs, gz_rs, local_sem,
    ag_ss, p1_rs, p2_rs, q1_rs, q2_rs, pair_rs,
    wg_ss, wgc_rs, wgz_rs, wx_rs, wy_rs, wf_rs, wl_rs,
):
    r, z = lax.axis_index("rows"), lax.axis_index("feat")
    core, x, y = lax.rem(r, 2), lax.rem(r // 2, SIDE), r // (2 * SIDE)

    def around(value, step):
        return lax.rem(value + step + 2 * SIDE, SIDE)

    def row_of(yy, xx, cc):
        return (yy * SIDE + xx) * 2 + cc

    place = ((x, y), (y, x))
    msg = (msg_a, msg_b)
    grads = (grads_a, grads_b)

    def owner(h, u, v, cc):
        return row_of(v, u, cc) if h == 0 else row_of(u, v, cc)

    def near(h, du, dv):
        u, v = place[h]
        return {"rows": owner(h, around(u, du), around(v, dv), core), "feat": z}

    sibling = {"rows": row_of(y, x, 1 - core), "feat": z}

    def along_z(d):
        return lax.rem(z + d, FEAT)

    def send(src, dst, ss, rs, target):
        pltpu.make_async_remote_copy(
            src_ref=src, dst_ref=dst, send_sem=ss, recv_sem=rs, device_id=target, device_id_type=MESH
        ).start()

    def loop(n, body, start=0):
        lax.fori_loop(start, n, lambda i, c: (body(i), c)[1], 0)

    def others(body):
        loop(FEAT, lambda d: body(along_z(d)), 1)

    barrier = pltpu.get_barrier_semaphore()
    partners = [sibling]
    for d in range(1, SIDE):
        partners += [near(0, d, 0), near(1, d, 0)]
    for d in range(1, FEAT):
        partners.append({"rows": r, "feat": along_z(d)})
    for target in partners:
        pl.semaphore_signal(barrier, inc=1, device_id=target, device_id_type=MESH)

    def inc_copy(g, b):
        return pltpu.make_async_copy(
            inc.at[pl.ds(b * GROUP, GROUP), :, pl.ds(g * CHUNK, CHUNK)],
            inc_buf.at[pl.ds((g * BATCHES + b) * GROUP, GROUP)],
            inc_sem.at[g * BATCHES + b],
        )

    for g in range(2):
        for b in range(BATCHES):
            inc_copy(g, b).start()

    lane = lax.broadcasted_iota(jnp.int32, (1, BLOCKS), 1)
    count = jnp.zeros((1, BLOCKS), jnp.int32)
    spots = [jnp.full((1, BLOCKS), NONE, jnp.int32) for _ in range(CAP)]
    for p in range(PAIRS):
        hit = lane == label_ref[p]
        spots = [jnp.where(hit & (count == k), p, spots[k]) for k in range(CAP)]
        count = count + jnp.where(hit, 1, 0)
    tab[...] = jnp.full(tab.shape, NONE, jnp.int32)
    tab_out[...] = jnp.full(tab.shape, NONE, jnp.int32)
    for k in range(CAP):
        tab[k : k + 1, :] = spots[k]
        tab_out[k : k + 1, :] = jnp.where(spots[k] < NONE, spots[k] + PAIRS, NONE)
    own_tab = pltpu.make_async_copy(tab, tab_own, tab_sems.at[0])
    own_tab.start()
    for t in range(feat.shape[1] // TILE):
        tiles[t] = feat[:, t * TILE : (t + 1) * TILE]
    for g in range(2):
        msg[g][NONE] = jnp.zeros((W, CHUNK), bf16)

    pl.semaphore_wait(barrier, len(partners))
    send(tab_out, tab_in, tab_sems.at[1], tab_sems.at[2], sibling)

    tile_count = feat.shape[1] // TILE

    def messages(g):
        def batch(b):
            inc_copy(g, b).wait()
            for k in range(GROUP):
                p = b * GROUP + k
                product = jnp.dot(
                    tiles[lax.rem(doc_ref[p], tile_count)], inc_buf[g * PAIRS + p], preferred_element_type=f32
                )
                msg[g][p] = (message_scale * product).astype(bf16)
            send(
                msg[g].at[pl.ds(b * GROUP, GROUP)], msg[g].at[pl.ds(PAIRS + b * GROUP, GROUP)],
                sib_ss.at[g], sib_rs.at[g * BATCHES + b], sibling,
            )

        loop(BATCHES, batch)

    def pair_messages_in(g):
        def one(b):
            wait(msg[g].at[pl.ds(PAIRS + b * GROUP, GROUP)], sib_rs.at[g * BATCHES + b])

        loop(BATCHES, one)

    def block_id(h, u, v, j, cc):
        return owner(h, u, v, cc) * LB + 2 * h + j

    def part(g, h, du, dv, j):
        u, v = place[h]
        block = block_id(h, around(u, du), around(v, dv), j, core)
        total = msg[g][tab_own[0, block]].astype(f32)
        for k in range(1, CAP):
            total = total + msg[g][tab_own[k, block]].astype(f32)
        for k in range(CAP):
            total = total + msg[g][tab_sib[k, block]].astype(f32)
        return total

    def slot(g, a, i, h, j):
        return (((a * 2 + g) * SIDE + i) * 2 + h) * 2 + j

    def far(g):
        def one(i):
            for h in range(2):
                for j in range(2):
                    k = slot(g, 0, i, h, j)
                    s1_send[k] = part(g, h, 2, offset(i), j).astype(bf16)
                    send(s1_send.at[k], s1_recv.at[k], s1_ss, s1_rs.at[k], near(h, 1 - 2 * j, 0))

        loop(SIDE, one)

    def close(g, passed):
        def one(i):
            for h in range(2):
                for way in range(2):
                    du = 1 - 2 * way
                    j = way if passed else 1 - way
                    k = slot(g, way, i, h, j)
                    total = part(g, h, du, offset(i), j)
                    if passed:
                        q = slot(g, 0, i, h, j)
                        wait(s1_recv.at[q], s1_rs.at[q])
                        total = total + s1_recv[q].astype(f32)
                    s2_send[k] = total.astype(bf16)
                    send(s2_send.at[k], s2_recv.at[k], s2_ss, s2_rs.at[k], near(h, du, 0))

        loop(SIDE, one)

    def column(g, i, h, j):
        total = part(g, h, 0, offset(i), j)
        for way in (1 - j, j):
            k = slot(g, way, i, h, j)
            wait(s2_recv.at[k], s2_rs.at[k])
            total = total + s2_recv[k].astype(f32)
        return total

    def four(way, h, j):
        return (way * 2 + h) * 2 + j

    def second_axis_sums(g):
        for h in range(2):
            for j in range(2):
                k = 4 * g + 2 * h + j
                t1_send[k] = column(g, 0, h, j).astype(bf16)
                send(t1_send.at[k], t1_recv.at[k], t_ss.at[0], t1_rs.at[k], near(h, 0, 1 - 2 * j))
        for passed in (False, True):
            for way in range(2):
                for h in range(2):
                    j = way if passed else 1 - way
                    k = 8 * g + four(way, h, j)
                    total = column(g, 1 + way, h, j)
                    if passed:
                        q = 4 * g + 2 * h + j
                        wait(t1_recv.at[q], t1_rs.at[q])
                        total = total + t1_recv[q].astype(f32)
                    t2_send[k] = total.astype(bf16)
                    send(t2_send.at[k], t2_recv.at[k], t_ss.at[1], t2_rs.at[k], near(h, 0, 1 - 2 * way))

    own_rows = pl.ds(pl.multiple_of(z * W, W), W)

    def rows_at(zz):
        return pl.ds(pl.multiple_of(zz * W, W), W)

    def lanes_in_block(zz, base=0):
        return pl.ds(pl.multiple_of(base + lax.rem(zz, 2) * PART, PART), PART)

    def lanes_in_all(zz, g):
        return pl.ds(pl.multiple_of((zz // 2) * TILE + g * CHUNK + lax.rem(zz, 2) * PART, PART), PART)

    def group_lanes(g):
        return pl.ds(g * PART, PART)

    def to(zz):
        return {"rows": r, "feat": zz}

    def finish_sums(g):
        for h in range(2):
            for j in range(2):
                total = column(g, 3, h, j)
                for way in (1 - j, j):
                    k = 8 * g + four(way, h, j)
                    wait(t2_recv.at[k], t2_rs.at[k])
                    total = total + t2_recv[k].astype(f32)
                summed[g * LB + 2 * h + j] = total.astype(bf16)

        def one(zz):
            send(summed.at[g * LB + zz // 2, :, lanes_in_block(zz)], xin.at[own_rows, group_lanes(g)],
                 z_ss.at[2], x_rs.at[g * FEAT + z], to(zz))

        others(one)
        xin[own_rows, group_lanes(g)] = summed[g * LB + z // 2, :, lanes_in_block(z)]

    half_cols = pl.ds(pl.multiple_of(core * (D // 2), D // 2), D // 2)
    other_cols = pl.ds(pl.multiple_of((1 - core) * (D // 2), D // 2), D // 2)

    def weight_start():
        others(lambda zz: send(weight.at[:, half_cols], wfull.at[own_rows, half_cols], z_ss.at[0], w_rs.at[z], to(zz)))
        wfull[own_rows, :] = weight[...]

    def weight_share():
        def one(zz):
            half = wfull.at[rows_at(zz), half_cols]
            wait(half, w_rs.at[zz])
            send(half, half, z_ss.at[5], w_rs.at[FEAT + zz], sibling)

        others(one)

    def spread_cotangent():
        def one(zz):
            for g in range(2):
                send(cot.at[:, lanes_in_all(zz, g)], cot_in.at[own_rows, group_lanes(g)],
                     z_ss.at[1], cot_rs.at[g * FEAT + z], to(zz))

        others(one)
        for g in range(2):
            cot_in[own_rows, group_lanes(g)] = cot[:, lanes_in_all(z, g)]

    own_copies = []

    def mix(g):
        if g == 0:
            others(lambda zz: wait(wfull.at[rows_at(zz), other_cols], w_rs.at[FEAT + zz]))

            def flip(o):
                rows = pl.ds(pl.multiple_of(o * CHUNK, CHUNK), CHUNK)
                wflip[rows, :] = wfull[:, rows].T

            loop(D // CHUNK, flip)
            for gg in range(2):
                others(lambda zz: wait(cot_in.at[rows_at(zz), group_lanes(gg)], cot_rs.at[gg * FEAT + zz]))
        others(lambda zz: wait(xin.at[rows_at(zz), group_lanes(g)], x_rs.at[g * FEAT + zz]))

        def forth(o):
            rows = pl.ds(pl.multiple_of(o * CHUNK, CHUNK), CHUNK)
            mixed = jnp.dot(wflip[rows, :], xin[:, group_lanes(g)], preferred_element_type=f32)
            gate = jax.nn.sigmoid(mixed)
            act_buf[rows, group_lanes(g)] = (mixed * gate).astype(bf16)
            slope = gate * (1.0 + mixed * (1.0 - gate))
            gm_buf[rows, group_lanes(g)] = (cot_in[rows, group_lanes(g)].astype(f32) * slope).astype(bf16)

        loop(D // CHUNK, forth)

        def back(o):
            rows = pl.ds(pl.multiple_of(o * CHUNK, CHUNK), CHUNK)
            gmt_buf[rows, group_lanes(g)] = jnp.dot(
                wfull[rows, :], gm_buf[:, group_lanes(g)], preferred_element_type=f32
            ).astype(bf16)

        loop(D // CHUNK, back)
        mine = grads[g].at[r * LB + z // 2, :, lanes_in_block(z)]
        others(lambda zz: send(gmt_buf.at[rows_at(zz), group_lanes(g)], mine, z_ss.at[3], gz_rs.at[g * FEAT + z], to(zz)))
        own = pltpu.make_async_copy(gmt_buf.at[own_rows, group_lanes(g)], mine, local_sem.at[g])
        own.start()
        own_copies.append(own)

    own_acts = []

    def give_act(g):
        there = act_out.at[:, lanes_in_all(z, g)]
        others(lambda zz: send(act_buf.at[rows_at(zz), group_lanes(g)], there, z_ss.at[4], act_rs.at[g * FEAT + z], to(zz)))
        own_act = pltpu.make_async_copy(act_buf.at[own_rows, group_lanes(g)], there, local_sem.at[2 + g])
        own_act.start()
        own_acts.append(own_act)

    def share(g, block):
        send(grads[g].at[block], grads[g].at[block], ag_ss.at[g], pair_rs.at[g], sibling)

    def pass_on(g, block, rs, target):
        send(grads[g].at[block], grads[g].at[block], ag_ss.at[g], rs, target)

    def at(h, du, dv, j):
        u, v = place[h]
        return block_id(h, around(u, du), around(v, dv), j, core)

    def second_axis(g, n, du, h, j):
        for way in range(2):
            pass_on(g, at(h, du, 0, j), q1_rs.at[g * 32 + n * 8 + four(way, h, j)], near(h, 0, 1 - 2 * way))

    def gather_own(g):
        own_copies[g].wait()
        others(lambda zz: wait(grads[g].at[r * LB + zz // 2, :, lanes_in_block(zz)], gz_rs.at[g * FEAT + zz]))
        for way in range(2):
            for h in range(2):
                for j in (way, 1 - way):
                    pass_on(g, at(h, 0, 0, j), p1_rs.at[8 * g + four(way, h, j)], near(h, 1 - 2 * way, 0))
        for h in range(2):
            for j in range(2):
                second_axis(g, 0, 0, h, j)
                share(g, at(h, 0, 0, j))

    def gather_near(g):
        for turn in range(2):
            for way in range(2):
                j = way if turn == 0 else 1 - way
                du = 2 * way - 1
                for h in range(2):
                    block = at(h, du, 0, j)
                    wait(grads[g].at[block], p1_rs.at[8 * g + four(way, h, j)])
                    if j == way:
                        pass_on(g, block, p2_rs.at[4 * g + 2 * h + way], near(h, 1 - 2 * way, 0))
                    second_axis(g, 1 + way, du, h, j)
                    share(g, block)

    def gather_far(g):
        for h in range(2):
            for j in range(2):
                block = at(h, 2, 0, j)
                wait(grads[g].at[block], p2_rs.at[4 * g + 2 * h + j])
                second_axis(g, 3, 2, h, j)
                share(g, block)

    offs = (0, -1, 1, 2)

    def take(g, n):
        for way in range(2):
            for h in range(2):
                for j in (way, 1 - way):
                    block = at(h, offs[n], 2 * way - 1, j)
                    wait(grads[g].at[block], q1_rs.at[g * 32 + n * 8 + four(way, h, j)])
                    if j == way:
                        pass_on(g, block, q2_rs.at[g * 16 + n * 4 + 2 * h + way], near(h, 0, 1 - 2 * way))
                    share(g, block)

    def take_last(g):
        for n in range(4):
            for h in range(2):
                for j in range(2):
                    block = at(h, offs[n], 2, j)
                    wait(grads[g].at[block], q2_rs.at[g * 16 + n * 4 + 2 * h + j])
                    share(g, block)

    def backward_ready(g):
        wait(grads[g].at[pl.ds(0, 64)], pair_rs.at[g])

    def backward(g, first, last):
        def batch(b):
            left, right = [], []
            for k in range(GROUP):
                p = b * GROUP + k
                grad = grads[g][label_ref[p]]
                tile = lax.rem(doc_ref[p], tile_count)
                left.append(
                    jnp.concatenate(
                        [jnp.where(tile == t, grad, jnp.zeros_like(grad)) for t in range(tile_count)], axis=0
                    )
                )
                right.append(inc_buf[g * PAIRS + p])
            fg_acc[...] += lax.dot_general(
                jnp.concatenate(left, axis=1), jnp.concatenate(right, axis=1),
                (((1,), (1,)), ((), ())), preferred_element_type=f32,
            )

        loop(last, batch, first)

    def backward_done():
        for t in range(tile_count):
            fg_out[:, t * TILE : (t + 1) * TILE] = fg_acc[t * W : (t + 1) * W, :].astype(bf16)

    HALF = W // 2

    def slab(s, cc):
        return pl.ds(pl.multiple_of(s * W + cc * HALF, HALF), HALF)

    def weight_inputs(g):
        lanes = group_lanes(g)
        send(xin.at[:, lanes], x_pair.at[:, lanes], wg_ss.at[0], wgc_rs.at[2 * g], sibling)
        send(gm_buf.at[:, lanes], gm_pair.at[:, lanes], wg_ss.at[0], wgc_rs.at[2 * g + 1], sibling)

    def weight_to_z():
        for g in range(2):
            wait(x_pair.at[:, group_lanes(g)], wgc_rs.at[2 * g])
            wait(gm_pair.at[:, group_lanes(g)], wgc_rs.at[2 * g + 1])

        lefts = [
            jnp.concatenate([left[slab(s, core), :] for s in range(FEAT)], axis=0) for left in (xin, x_pair)
        ]
        for n in range(D // CHUNK):
            columns = slice(n * CHUNK, (n + 1) * CHUNK)
            total = 0
            for left, right in zip(lefts, (gm_buf, gm_pair)):
                total = total + lax.dot_general(
                    left, right[columns, :], (((1,), (1,)), ((), ())), preferred_element_type=f32
                )
            for s in range(FEAT):
                wgz_send[s, :, columns] = total[s * HALF : (s + 1) * HALF].astype(bf16)

        others(lambda zz: send(wgz_send.at[zz], wgz_recv.at[z], wg_ss.at[1], wgz_rs.at[z], to(zz)))
        wg_half[...] = wgz_send[z].astype(f32)

    def weight_to_x():
        def one(zz):
            wait(wgz_recv.at[zz], wgz_rs.at[zz])
            wg_half[...] += wgz_recv[zz].astype(f32)

        others(one)
        for t in range(36):
            a, b = t // 6, t % 6
            wx_send[t // 9, t % 9] = wg_half[8 * a : 8 * a + 8, 128 * b : 128 * b + 128]
        for d in range(1, SIDE):
            xx = around(x, d)
            send(wx_send.at[xx], wx_recv.at[x], wg_ss.at[2], wx_rs.at[x], near(0, d, 0))

    def weight_to_y():
        total = wx_send[x]
        for d in range(1, SIDE):
            xx = around(x, d)
            wait(wx_recv.at[xx], wx_rs.at[xx])
            total = total + wx_recv[xx]
        wy_send[...] = total
        wy_recv[y] = total
        for d in range(1, SIDE):
            send(wy_send, wy_recv.at[y], wg_ss.at[3], wy_rs.at[y], near(1, d, 0))

    def weight_back_x():
        for d in range(1, SIDE):
            yy = around(y, d)
            wait(wy_recv.at[yy], wy_rs.at[yy])
        total = (wy_recv[0] + wy_recv[1]) + (wy_recv[2] + wy_recv[3])
        wf_send[...] = total
        wf_recv[x] = total
        for d in range(1, SIDE):
            send(wf_send, wf_recv.at[x], wg_ss.at[4], wf_rs.at[x], near(0, d, 0))

    mine = pl.ds(pl.multiple_of(core * HALF, HALF), HALF)
    other = pl.ds(pl.multiple_of((1 - core) * HALF, HALF), HALF)
    own_wg = pltpu.make_async_copy(wg_half, wg_out.at[mine, :], local_sem.at[4])

    def weight_done():
        for d in range(1, SIDE):
            xx = around(x, d)
            wait(wf_recv.at[xx], wf_rs.at[xx])
        for t in range(36):
            a, b = t // 6, t % 6
            wg_half[8 * a : 8 * a + 8, 128 * b : 128 * b + 128] = wf_recv[t // 9, t % 9]
        send(wg_half, wg_out.at[mine, :], wg_ss.at[5], wl_rs, sibling)
        own_wg.start()

    weight_start()
    spread_cotangent()
    messages(0)
    wait(tab_in, tab_sems.at[2])
    sib_tab = pltpu.make_async_copy(tab_in, tab_sib, tab_sems.at[3])
    sib_tab.start()
    own_tab.wait()
    sib_tab.wait()
    pair_messages_in(0)
    far(0)
    close(0, False)
    messages(1)
    close(0, True)
    second_axis_sums(0)
    pair_messages_in(1)
    far(1)
    close(1, False)
    finish_sums(0)
    close(1, True)
    weight_share()
    mix(0)
    second_axis_sums(1)
    gather_own(0)
    finish_sums(1)
    give_act(0)
    gather_near(0)
    weight_inputs(0)
    gather_far(0)
    mix(1)
    weight_inputs(1)
    take(0, 0)
    take(0, 1)
    take(0, 2)
    weight_to_z()
    take(0, 3)
    gather_own(1)
    give_act(1)
    fg_acc[...] = jnp.zeros_like(fg_acc)
    take_last(0)
    gather_near(1)
    gather_far(1)
    backward_ready(0)
    backward(0, 0, 3)
    take(1, 0)
    backward(0, 3, 6)
    take(1, 1)
    take(1, 2)
    weight_to_x()
    take(1, 3)
    weight_to_y()
    take_last(1)
    weight_back_x()
    backward_ready(1)
    backward(1, 0, 3)
    weight_done()
    backward(1, 3, BATCHES)
    backward_done()

    own_wg.wait()
    wait(wg_out.at[other, :], wl_rs)
    for g in range(2):
        own_acts[g].wait()
        others(lambda zz: wait(act_out.at[:, lanes_in_all(zz, g)], act_rs.at[g * FEAT + zz]))
    for g in range(2):
        wait(msg[g].at[pl.ds(0, PAIRS)], sib_ss.at[g])
        wait(grads[g].at[pl.ds(0, 124)], ag_ss.at[g])
    wait(tab_out, tab_sems.at[1])
    wait(s1_send, s1_ss)
    wait(s2_send, s2_ss)
    wait(t1_send, t_ss.at[0])
    wait(t2_send, t_ss.at[1])
    seven = pl.ds(0, (FEAT - 1) * W)
    for k in (0, 5):
        wait(wfull.at[seven, half_cols], z_ss.at[k])
    for k in range(1, 5):
        wait(cot_in.at[seven, :], z_ss.at[k])
    wait(wfull.at[:, pl.ds(0, 2 * CHUNK)], wg_ss.at[0])
    wait(wgz_send.at[pl.ds(0, FEAT - 1)], wg_ss.at[1])
    for k in (2, 3, 4):
        wait(wx_send.at[pl.ds(0, SIDE - 1)], wg_ss.at[k])
    wait(wg_half, wg_ss.at[5])


def exchange(doc, label, feat, inc, weight, cot):
    dma = pltpu.SemaphoreType.DMA
    block = (W, CHUNK)
    vmem = pltpu.VMEM
    smem_spec = pl.BlockSpec(memory_space=pltpu.SMEM)
    any_spec = pl.BlockSpec(memory_space=pl.ANY)
    vmem_spec = pl.BlockSpec(memory_space=pltpu.VMEM)
    table = ((8, BLOCKS), jnp.int32)
    return pl.pallas_call(
        exchange_kernel,
        in_specs=[smem_spec, smem_spec, vmem_spec, any_spec, vmem_spec, vmem_spec],
        out_specs=[any_spec, any_spec, vmem_spec],
        out_shape=[
            jax.ShapeDtypeStruct(cot.shape, bf16),
            jax.ShapeDtypeStruct((W, D), f32),
            jax.ShapeDtypeStruct(feat.shape, bf16),
        ],
        scratch_shapes=[
            vmem((BLOCKS, *block), bf16), vmem((BLOCKS, *block), bf16),
            vmem((feat.shape[1] // TILE * W, TILE), f32),
            vmem((feat.shape[1] // TILE, W, TILE), bf16),
            vmem((2 * PAIRS, TILE, CHUNK), bf16), vmem((NONE + 1, *block), bf16), vmem((NONE + 1, *block), bf16),
            vmem(*table), vmem(*table), vmem(*table), pltpu.SMEM(*table), pltpu.SMEM(*table),
            vmem((32, *block), bf16), vmem((32, *block), bf16),
            vmem((64, *block), bf16), vmem((64, *block), bf16),
            vmem((8, *block), bf16), vmem((8, *block), bf16),
            vmem((16, *block), bf16), vmem((16, *block), bf16),
            vmem((2 * LB, *block), bf16),
            vmem((D, CHUNK), bf16), vmem((D, D), bf16), vmem((D, CHUNK), bf16),
            vmem((D, CHUNK), bf16), vmem((D, CHUNK), bf16), vmem((D, CHUNK), bf16),
            vmem((D, D), bf16), vmem((D, CHUNK), bf16), vmem((D, CHUNK), bf16),
            vmem((FEAT, W // 2, D), bf16), vmem((FEAT, W // 2, D), bf16),
            vmem((SIDE, 9, 8, 128), f32), vmem((SIDE, 9, 8, 128), f32),
            vmem((9, 8, 128), f32), vmem((SIDE, 9, 8, 128), f32),
            vmem((9, 8, 128), f32), vmem((SIDE, 9, 8, 128), f32),
            vmem((W // 2, D), f32),
            dma((2 * BATCHES,)), dma((4,)), dma((2,)), dma((2 * BATCHES,)),
            dma, dma((32,)), dma, dma((64,)), dma((2,)), dma((8,)), dma((16,)),
            dma((6,)), dma((2 * FEAT,)), dma((2 * FEAT,)), dma((2 * FEAT,)), dma((2 * FEAT,)), dma((2 * FEAT,)), dma((5,)),
            dma((2,)), dma((16,)), dma((8,)), dma((64,)), dma((32,)), dma((2,)),
            dma((6,)), dma((4,)), dma((FEAT,)), dma((SIDE,)), dma((SIDE,)), dma((SIDE,)), dma,
        ],
        compiler_params=pltpu.CompilerParams(
            collective_id=0, has_side_effects=True, vmem_limit_bytes=VMEM_LIMIT
        ),
    )(doc, label, feat, inc, weight, cot)


def results_kernel(*refs):
    half = len(refs) // 2
    ins, outs, sems = refs[:half], refs[half : 2 * half], refs[-1]
    copies = [pltpu.make_async_copy(i, o, sems.at[k]) for k, (i, o) in enumerate(zip(ins, outs))]
    for copy in copies:
        copy.start()
    for copy in copies:
        copy.wait()


def results(*arrays):
    return pl.pallas_call(
        results_kernel,
        in_specs=[pl.BlockSpec(memory_space=pl.ANY)] * len(arrays),
        out_specs=[pl.BlockSpec(memory_space=pltpu.VMEM)] * len(arrays),
        out_shape=[jax.ShapeDtypeStruct(a.shape, a.dtype) for a in arrays],
        scratch_shapes=[pltpu.SemaphoreType.DMA((len(arrays),))],
    )(*arrays)


def local(features, pair_doc, pair_label, incidence, weight, cotangent):
    act, weight_grad, feature_grad = results(
        *exchange(pair_doc, pair_label, features.T, incidence, weight, cotangent.T)
    )
    return act.T, weight_grad, feature_grad.T


def solution(mesh):
    return jax.shard_map(
        local,
        mesh=mesh,
        in_specs=(
            P("rows", "feat"),
            P("rows"),
            P("rows"),
            P("rows", None, None),
            P("feat", None),
            P("rows", "feat"),
        ),
        out_specs=(P("rows", "feat"), P("feat", None), P("rows", "feat")),
        check_vma=False,
    )
```

```python
import functools

import jax
import jax.numpy as jnp
from jax import lax
from jax.experimental import pallas as pl
from jax.experimental.pallas import tpu as pltpu
from jax.sharding import PartitionSpec as P

MESH = pl.DeviceIdType.MESH
message_scale = 0.0625

SIDE = 4
FEAT = 8
LB = 4
CAP = 3
TILE = 512
PAIRS = 24
W = 96
D = 768
GROUP = 4
BLOCKS = 128
CHUNK = 256
PART = 128
BATCHES = PAIRS // GROUP
NONE = 2 * PAIRS
VMEM_LIMIT = 60 * 1024 * 1024

f32, bf16 = jnp.float32, jnp.bfloat16


def wait(ref, sem):
    pltpu.make_async_copy(ref, ref, sem).wait()


def offset(i):
    return 2 - i + 3 * (i // 2) - 2 * (i // 3)


def exchange_kernel(
    doc_ref, label_ref, feat, inc, weight, cot,
    act_out, wg_out, fg_out,
    grads_a, grads_b, fg_acc,
    tiles, inc_buf, msg_a, msg_b, tab, tab_out, tab_in, tab_own, tab_sib,
    s1_send, s1_recv, s2_send, s2_recv, t1_send, t1_recv, t2_send, t2_recv,
    summed, xin, wfull, cot_in, act_buf, gm_buf, gmt_buf,
    wflip, x_pair, gm_pair, wgz_send, wgz_recv, wx_send, wx_recv, wy_send, wy_recv, wf_send, wf_recv, wg_half,
    inc_sem, tab_sems, sib_ss, sib_rs, s1_ss, s1_rs, s2_ss, s2_rs, t_ss, t1_rs, t2_rs,
    z_ss, x_rs, w_rs, cot_rs, act_rs, gz_rs, local_sem,
    ag_ss, p1_rs, p2_rs, q1_rs, q2_rs, pair_rs,
    wg_ss, wgc_rs, wgz_rs, wx_rs, wy_rs, wf_rs, wl_rs,
):
    r, z = lax.axis_index("rows"), lax.axis_index("feat")
    core, x, y = lax.rem(r, 2), lax.rem(r // 2, SIDE), r // (2 * SIDE)

    def around(value, step):
        return lax.rem(value + step + 2 * SIDE, SIDE)

    def row_of(yy, xx, cc):
        return (yy * SIDE + xx) * 2 + cc

    place = ((x, y), (y, x))
    msg = (msg_a, msg_b)
    grads = (grads_a, grads_b)

    def owner(h, u, v, cc):
        return row_of(v, u, cc) if h == 0 else row_of(u, v, cc)

    def near(h, du, dv):
        u, v = place[h]
        return {"rows": owner(h, around(u, du), around(v, dv), core), "feat": z}

    sibling = {"rows": row_of(y, x, 1 - core), "feat": z}

    def along_z(d):
        return lax.rem(z + d, FEAT)

    def send(src, dst, ss, rs, target):
        pltpu.make_async_remote_copy(
            src_ref=src, dst_ref=dst, send_sem=ss, recv_sem=rs, device_id=target, device_id_type=MESH
        ).start()

    def loop(n, body, start=0):
        lax.fori_loop(start, n, lambda i, c: (body(i), c)[1], 0)

    def others(body):
        loop(FEAT, lambda d: body(along_z(d)), 1)

    barrier = pltpu.get_barrier_semaphore()
    partners = [sibling]
    for d in range(1, SIDE):
        partners += [near(0, d, 0), near(1, d, 0)]
    for d in range(1, FEAT):
        partners.append({"rows": r, "feat": along_z(d)})
    for target in partners:
        pl.semaphore_signal(barrier, inc=1, device_id=target, device_id_type=MESH)

    def inc_copy(g, b):
        return pltpu.make_async_copy(
            inc.at[pl.ds(b * GROUP, GROUP), :, pl.ds(g * CHUNK, CHUNK)],
            inc_buf.at[pl.ds((g * BATCHES + b) * GROUP, GROUP)],
            inc_sem.at[g * BATCHES + b],
        )

    for g in range(2):
        for b in range(BATCHES):
            inc_copy(g, b).start()

    lane = lax.broadcasted_iota(jnp.int32, (1, BLOCKS), 1)
    count = jnp.zeros((1, BLOCKS), jnp.int32)
    spots = [jnp.full((1, BLOCKS), NONE, jnp.int32) for _ in range(CAP)]
    for p in range(PAIRS):
        hit = lane == label_ref[p]
        spots = [jnp.where(hit & (count == k), p, spots[k]) for k in range(CAP)]
        count = count + jnp.where(hit, 1, 0)
    tab[...] = jnp.full(tab.shape, NONE, jnp.int32)
    tab_out[...] = jnp.full(tab.shape, NONE, jnp.int32)
    for k in range(CAP):
        tab[k : k + 1, :] = spots[k]
        tab_out[k : k + 1, :] = jnp.where(spots[k] < NONE, spots[k] + PAIRS, NONE)
    own_tab = pltpu.make_async_copy(tab, tab_own, tab_sems.at[0])
    own_tab.start()
    for t in range(feat.shape[1] // TILE):
        tiles[t] = feat[:, t * TILE : (t + 1) * TILE]
    for g in range(2):
        msg[g][NONE] = jnp.zeros((W, CHUNK), bf16)

    pl.semaphore_wait(barrier, len(partners))
    send(tab_out, tab_in, tab_sems.at[1], tab_sems.at[2], sibling)

    tile_count = feat.shape[1] // TILE

    def messages(g):
        def batch(b):
            inc_copy(g, b).wait()
            for k in range(GROUP):
                p = b * GROUP + k
                product = jnp.dot(
                    tiles[lax.rem(doc_ref[p], tile_count)], inc_buf[g * PAIRS + p], preferred_element_type=f32
                )
                msg[g][p] = (message_scale * product).astype(bf16)
            send(
                msg[g].at[pl.ds(b * GROUP, GROUP)], msg[g].at[pl.ds(PAIRS + b * GROUP, GROUP)],
                sib_ss.at[g], sib_rs.at[g * BATCHES + b], sibling,
            )

        loop(BATCHES, batch)

    def pair_messages_in(g):
        def one(b):
            wait(msg[g].at[pl.ds(PAIRS + b * GROUP, GROUP)], sib_rs.at[g * BATCHES + b])

        loop(BATCHES, one)

    def block_id(h, u, v, j, cc):
        return owner(h, u, v, cc) * LB + 2 * h + j

    def part(g, h, du, dv, j):
        u, v = place[h]
        block = block_id(h, around(u, du), around(v, dv), j, core)
        total = msg[g][tab_own[0, block]].astype(f32)
        for k in range(1, CAP):
            total = total + msg[g][tab_own[k, block]].astype(f32)
        for k in range(CAP):
            total = total + msg[g][tab_sib[k, block]].astype(f32)
        return total

    def slot(g, a, i, h, j):
        return (((a * 2 + g) * SIDE + i) * 2 + h) * 2 + j

    def far(g):
        def one(i):
            for h in range(2):
                for j in range(2):
                    k = slot(g, 0, i, h, j)
                    s1_send[k] = part(g, h, 2, offset(i), j).astype(bf16)
                    send(s1_send.at[k], s1_recv.at[k], s1_ss, s1_rs.at[k], near(h, 1 - 2 * j, 0))

        loop(SIDE, one)

    def close(g, passed):
        def one(i):
            for h in range(2):
                for way in range(2):
                    du = 1 - 2 * way
                    j = way if passed else 1 - way
                    k = slot(g, way, i, h, j)
                    total = part(g, h, du, offset(i), j)
                    if passed:
                        q = slot(g, 0, i, h, j)
                        wait(s1_recv.at[q], s1_rs.at[q])
                        total = total + s1_recv[q].astype(f32)
                    s2_send[k] = total.astype(bf16)
                    send(s2_send.at[k], s2_recv.at[k], s2_ss, s2_rs.at[k], near(h, du, 0))

        loop(SIDE, one)

    def column(g, i, h, j):
        total = part(g, h, 0, offset(i), j)
        for way in (1 - j, j):
            k = slot(g, way, i, h, j)
            wait(s2_recv.at[k], s2_rs.at[k])
            total = total + s2_recv[k].astype(f32)
        return total

    def four(way, h, j):
        return (way * 2 + h) * 2 + j

    def second_axis_sums(g):
        for h in range(2):
            for j in range(2):
                k = 4 * g + 2 * h + j
                t1_send[k] = column(g, 0, h, j).astype(bf16)
                send(t1_send.at[k], t1_recv.at[k], t_ss.at[0], t1_rs.at[k], near(h, 0, 1 - 2 * j))
        for passed in (False, True):
            for way in range(2):
                for h in range(2):
                    j = way if passed else 1 - way
                    k = 8 * g + four(way, h, j)
                    total = column(g, 1 + way, h, j)
                    if passed:
                        q = 4 * g + 2 * h + j
                        wait(t1_recv.at[q], t1_rs.at[q])
                        total = total + t1_recv[q].astype(f32)
                    t2_send[k] = total.astype(bf16)
                    send(t2_send.at[k], t2_recv.at[k], t_ss.at[1], t2_rs.at[k], near(h, 0, 1 - 2 * way))

    own_rows = pl.ds(pl.multiple_of(z * W, W), W)

    def rows_at(zz):
        return pl.ds(pl.multiple_of(zz * W, W), W)

    def lanes_in_block(zz, base=0):
        return pl.ds(pl.multiple_of(base + lax.rem(zz, 2) * PART, PART), PART)

    def lanes_in_all(zz, g):
        return pl.ds(pl.multiple_of((zz // 2) * TILE + g * CHUNK + lax.rem(zz, 2) * PART, PART), PART)

    def group_lanes(g):
        return pl.ds(g * PART, PART)

    def to(zz):
        return {"rows": r, "feat": zz}

    def finish_sums(g):
        for h in range(2):
            for j in range(2):
                total = column(g, 3, h, j)
                for way in (1 - j, j):
                    k = 8 * g + four(way, h, j)
                    wait(t2_recv.at[k], t2_rs.at[k])
                    total = total + t2_recv[k].astype(f32)
                summed[g * LB + 2 * h + j] = total.astype(bf16)

        def one(zz):
            send(summed.at[g * LB + zz // 2, :, lanes_in_block(zz)], xin.at[own_rows, group_lanes(g)],
                 z_ss.at[2], x_rs.at[g * FEAT + z], to(zz))

        others(one)
        xin[own_rows, group_lanes(g)] = summed[g * LB + z // 2, :, lanes_in_block(z)]

    half_cols = pl.ds(pl.multiple_of(core * (D // 2), D // 2), D // 2)
    other_cols = pl.ds(pl.multiple_of((1 - core) * (D // 2), D // 2), D // 2)

    def weight_start():
        others(lambda zz: send(weight.at[:, half_cols], wfull.at[own_rows, half_cols], z_ss.at[0], w_rs.at[z], to(zz)))
        wfull[own_rows, :] = weight[...]

    def weight_share():
        def one(zz):
            half = wfull.at[rows_at(zz), half_cols]
            wait(half, w_rs.at[zz])
            send(half, half, z_ss.at[5], w_rs.at[FEAT + zz], sibling)

        others(one)

    def spread_cotangent():
        def one(zz):
            for g in range(2):
                send(cot.at[:, lanes_in_all(zz, g)], cot_in.at[own_rows, group_lanes(g)],
                     z_ss.at[1], cot_rs.at[g * FEAT + z], to(zz))

        others(one)
        for g in range(2):
            cot_in[own_rows, group_lanes(g)] = cot[:, lanes_in_all(z, g)]

    own_copies = []

    def mix(g):
        if g == 0:
            others(lambda zz: wait(wfull.at[rows_at(zz), other_cols], w_rs.at[FEAT + zz]))

            def flip(o):
                rows = pl.ds(pl.multiple_of(o * CHUNK, CHUNK), CHUNK)
                wflip[rows, :] = wfull[:, rows].T

            loop(D // CHUNK, flip)
            for gg in range(2):
                others(lambda zz: wait(cot_in.at[rows_at(zz), group_lanes(gg)], cot_rs.at[gg * FEAT + zz]))
        others(lambda zz: wait(xin.at[rows_at(zz), group_lanes(g)], x_rs.at[g * FEAT + zz]))

        def forth(o):
            rows = pl.ds(pl.multiple_of(o * CHUNK, CHUNK), CHUNK)
            mixed = jnp.dot(wflip[rows, :], xin[:, group_lanes(g)], preferred_element_type=f32)
            gate = jax.nn.sigmoid(mixed)
            act_buf[rows, group_lanes(g)] = (mixed * gate).astype(bf16)
            slope = gate * (1.0 + mixed * (1.0 - gate))
            gm_buf[rows, group_lanes(g)] = (cot_in[rows, group_lanes(g)].astype(f32) * slope).astype(bf16)

        loop(D // CHUNK, forth)

        def back(o):
            rows = pl.ds(pl.multiple_of(o * CHUNK, CHUNK), CHUNK)
            gmt_buf[rows, group_lanes(g)] = jnp.dot(
                wfull[rows, :], gm_buf[:, group_lanes(g)], preferred_element_type=f32
            ).astype(bf16)

        loop(D // CHUNK, back)
        mine = grads[g].at[r * LB + z // 2, :, lanes_in_block(z)]
        others(lambda zz: send(gmt_buf.at[rows_at(zz), group_lanes(g)], mine, z_ss.at[3], gz_rs.at[g * FEAT + z], to(zz)))
        own = pltpu.make_async_copy(gmt_buf.at[own_rows, group_lanes(g)], mine, local_sem.at[g])
        own.start()
        own_copies.append(own)

    own_acts = []

    def give_act(g):
        there = act_out.at[:, lanes_in_all(z, g)]
        others(lambda zz: send(act_buf.at[rows_at(zz), group_lanes(g)], there, z_ss.at[4], act_rs.at[g * FEAT + z], to(zz)))
        own_act = pltpu.make_async_copy(act_buf.at[own_rows, group_lanes(g)], there, local_sem.at[2 + g])
        own_act.start()
        own_acts.append(own_act)

    def share(g, block):
        send(grads[g].at[block], grads[g].at[block], ag_ss.at[g], pair_rs.at[g], sibling)

    def pass_on(g, block, rs, target):
        send(grads[g].at[block], grads[g].at[block], ag_ss.at[g], rs, target)

    def at(h, du, dv, j):
        u, v = place[h]
        return block_id(h, around(u, du), around(v, dv), j, core)

    def second_axis(g, n, du, h, j):
        for way in range(2):
            pass_on(g, at(h, du, 0, j), q1_rs.at[g * 32 + n * 8 + four(way, h, j)], near(h, 0, 1 - 2 * way))

    def gather_own(g):
        own_copies[g].wait()
        others(lambda zz: wait(grads[g].at[r * LB + zz // 2, :, lanes_in_block(zz)], gz_rs.at[g * FEAT + zz]))
        for way in range(2):
            for h in range(2):
                for j in (way, 1 - way):
                    pass_on(g, at(h, 0, 0, j), p1_rs.at[8 * g + four(way, h, j)], near(h, 1 - 2 * way, 0))
        for h in range(2):
            for j in range(2):
                second_axis(g, 0, 0, h, j)
                share(g, at(h, 0, 0, j))

    def gather_near(g):
        for turn in range(2):
            for way in range(2):
                j = way if turn == 0 else 1 - way
                du = 2 * way - 1
                for h in range(2):
                    block = at(h, du, 0, j)
                    wait(grads[g].at[block], p1_rs.at[8 * g + four(way, h, j)])
                    if j == way:
                        pass_on(g, block, p2_rs.at[4 * g + 2 * h + way], near(h, 1 - 2 * way, 0))
                    second_axis(g, 1 + way, du, h, j)
                    share(g, block)

    def gather_far(g):
        for h in range(2):
            for j in range(2):
                block = at(h, 2, 0, j)
                wait(grads[g].at[block], p2_rs.at[4 * g + 2 * h + j])
                second_axis(g, 3, 2, h, j)
                share(g, block)

    offs = (0, -1, 1, 2)

    def take(g, n):
        for way in range(2):
            for h in range(2):
                for j in (way, 1 - way):
                    block = at(h, offs[n], 2 * way - 1, j)
                    wait(grads[g].at[block], q1_rs.at[g * 32 + n * 8 + four(way, h, j)])
                    if j == way:
                        pass_on(g, block, q2_rs.at[g * 16 + n * 4 + 2 * h + way], near(h, 0, 1 - 2 * way))
                    share(g, block)

    def take_last(g):
        for n in range(4):
            for h in range(2):
                for j in range(2):
                    block = at(h, offs[n], 2, j)
                    wait(grads[g].at[block], q2_rs.at[g * 16 + n * 4 + 2 * h + j])
                    share(g, block)

    def backward_ready(g):
        wait(grads[g].at[pl.ds(0, 64)], pair_rs.at[g])

    def backward(g, first, last):
        def batch(b):
            left, right = [], []
            for k in range(GROUP):
                p = b * GROUP + k
                grad = grads[g][label_ref[p]]
                tile = lax.rem(doc_ref[p], tile_count)
                left.append(
                    jnp.concatenate(
                        [jnp.where(tile == t, grad, jnp.zeros_like(grad)) for t in range(tile_count)], axis=0
                    )
                )
                right.append(inc_buf[g * PAIRS + p])
            fg_acc[...] += lax.dot_general(
                jnp.concatenate(left, axis=1), jnp.concatenate(right, axis=1),
                (((1,), (1,)), ((), ())), preferred_element_type=f32,
            )

        loop(last, batch, first)

    def backward_done():
        for t in range(tile_count):
            fg_out[:, t * TILE : (t + 1) * TILE] = fg_acc[t * W : (t + 1) * W, :].astype(bf16)

    HALF = W // 2

    def slab(s, cc):
        return pl.ds(pl.multiple_of(s * W + cc * HALF, HALF), HALF)

    def weight_inputs(g):
        lanes = group_lanes(g)
        send(xin.at[:, lanes], x_pair.at[:, lanes], wg_ss.at[0], wgc_rs.at[2 * g], sibling)
        send(gm_buf.at[:, lanes], gm_pair.at[:, lanes], wg_ss.at[0], wgc_rs.at[2 * g + 1], sibling)

    def weight_to_z():
        for g in range(2):
            wait(x_pair.at[:, group_lanes(g)], wgc_rs.at[2 * g])
            wait(gm_pair.at[:, group_lanes(g)], wgc_rs.at[2 * g + 1])

        lefts = [
            jnp.concatenate([left[slab(s, core), :] for s in range(FEAT)], axis=0) for left in (xin, x_pair)
        ]
        for n in range(D // CHUNK):
            columns = slice(n * CHUNK, (n + 1) * CHUNK)
            total = 0
            for left, right in zip(lefts, (gm_buf, gm_pair)):
                total = total + lax.dot_general(
                    left, right[columns, :], (((1,), (1,)), ((), ())), preferred_element_type=f32
                )
            for s in range(FEAT):
                wgz_send[s, :, columns] = total[s * HALF : (s + 1) * HALF].astype(bf16)

        others(lambda zz: send(wgz_send.at[zz], wgz_recv.at[z], wg_ss.at[1], wgz_rs.at[z], to(zz)))
        wg_half[...] = wgz_send[z].astype(f32)

    def weight_to_x():
        def one(zz):
            wait(wgz_recv.at[zz], wgz_rs.at[zz])
            wg_half[...] += wgz_recv[zz].astype(f32)

        others(one)
        for t in range(36):
            a, b = t // 6, t % 6
            wx_send[t // 9, t % 9] = wg_half[8 * a : 8 * a + 8, 128 * b : 128 * b + 128]
        for d in range(1, SIDE):
            xx = around(x, d)
            send(wx_send.at[xx], wx_recv.at[x], wg_ss.at[2], wx_rs.at[x], near(0, d, 0))

    def weight_to_y():
        total = wx_send[x]
        for d in range(1, SIDE):
            xx = around(x, d)
            wait(wx_recv.at[xx], wx_rs.at[xx])
            total = total + wx_recv[xx]
        wy_send[...] = total
        wy_recv[y] = total
        for d in range(1, SIDE):
            send(wy_send, wy_recv.at[y], wg_ss.at[3], wy_rs.at[y], near(1, d, 0))

    def weight_back_x():
        for d in range(1, SIDE):
            yy = around(y, d)
            wait(wy_recv.at[yy], wy_rs.at[yy])
        total = (wy_recv[0] + wy_recv[1]) + (wy_recv[2] + wy_recv[3])
        wf_send[...] = total
        wf_recv[x] = total
        for d in range(1, SIDE):
            send(wf_send, wf_recv.at[x], wg_ss.at[4], wf_rs.at[x], near(0, d, 0))

    mine = pl.ds(pl.multiple_of(core * HALF, HALF), HALF)
    other = pl.ds(pl.multiple_of((1 - core) * HALF, HALF), HALF)
    own_wg = pltpu.make_async_copy(wg_half, wg_out.at[mine, :], local_sem.at[4])

    def weight_done():
        for d in range(1, SIDE):
            xx = around(x, d)
            wait(wf_recv.at[xx], wf_rs.at[xx])
        for t in range(36):
            a, b = t // 6, t % 6
            wg_half[8 * a : 8 * a + 8, 128 * b : 128 * b + 128] = wf_recv[t // 9, t % 9]
        send(wg_half, wg_out.at[mine, :], wg_ss.at[5], wl_rs, sibling)
        own_wg.start()

    weight_start()
    spread_cotangent()
    messages(0)
    wait(tab_in, tab_sems.at[2])
    sib_tab = pltpu.make_async_copy(tab_in, tab_sib, tab_sems.at[3])
    sib_tab.start()
    own_tab.wait()
    sib_tab.wait()
    pair_messages_in(0)
    far(0)
    close(0, False)
    messages(1)
    close(0, True)
    second_axis_sums(0)
    pair_messages_in(1)
    far(1)
    close(1, False)
    finish_sums(0)
    close(1, True)
    weight_share()
    mix(0)
    second_axis_sums(1)
    gather_own(0)
    finish_sums(1)
    give_act(0)
    gather_near(0)
    weight_inputs(0)
    gather_far(0)
    mix(1)
    weight_inputs(1)
    take(0, 0)
    take(0, 1)
    take(0, 2)
    weight_to_z()
    take(0, 3)
    gather_own(1)
    give_act(1)
    fg_acc[...] = jnp.zeros_like(fg_acc)
    take_last(0)
    gather_near(1)
    gather_far(1)
    take(1, 0)
    backward_ready(0)
    backward(0, 0, 2)
    take(1, 1)
    backward(0, 2, 4)
    take(1, 2)
    weight_to_x()
    backward(0, 4, 6)
    take(1, 3)
    weight_to_y()
    take_last(1)
    weight_back_x()
    backward_ready(1)
    backward(1, 0, 3)
    weight_done()
    backward(1, 3, BATCHES)
    backward_done()

    own_wg.wait()
    wait(wg_out.at[other, :], wl_rs)
    for g in range(2):
        own_acts[g].wait()
        others(lambda zz: wait(act_out.at[:, lanes_in_all(zz, g)], act_rs.at[g * FEAT + zz]))
    for g in range(2):
        wait(msg[g].at[pl.ds(0, PAIRS)], sib_ss.at[g])
        wait(grads[g].at[pl.ds(0, 124)], ag_ss.at[g])
    wait(tab_out, tab_sems.at[1])
    wait(s1_send, s1_ss)
    wait(s2_send, s2_ss)
    wait(t1_send, t_ss.at[0])
    wait(t2_send, t_ss.at[1])
    seven = pl.ds(0, (FEAT - 1) * W)
    for k in (0, 5):
        wait(wfull.at[seven, half_cols], z_ss.at[k])
    for k in range(1, 5):
        wait(cot_in.at[seven, :], z_ss.at[k])
    wait(wfull.at[:, pl.ds(0, 2 * CHUNK)], wg_ss.at[0])
    wait(wgz_send.at[pl.ds(0, FEAT - 1)], wg_ss.at[1])
    for k in (2, 3, 4):
        wait(wx_send.at[pl.ds(0, SIDE - 1)], wg_ss.at[k])
    wait(wg_half, wg_ss.at[5])


def exchange(doc, label, feat, inc, weight, cot):
    dma = pltpu.SemaphoreType.DMA
    block = (W, CHUNK)
    vmem = pltpu.VMEM
    smem_spec = pl.BlockSpec(memory_space=pltpu.SMEM)
    any_spec = pl.BlockSpec(memory_space=pl.ANY)
    vmem_spec = pl.BlockSpec(memory_space=pltpu.VMEM)
    table = ((8, BLOCKS), jnp.int32)
    return pl.pallas_call(
        exchange_kernel,
        in_specs=[smem_spec, smem_spec, vmem_spec, any_spec, vmem_spec, vmem_spec],
        out_specs=[any_spec, any_spec, vmem_spec],
        out_shape=[
            jax.ShapeDtypeStruct(cot.shape, bf16),
            jax.ShapeDtypeStruct((W, D), f32),
            jax.ShapeDtypeStruct(feat.shape, bf16),
        ],
        scratch_shapes=[
            vmem((BLOCKS, *block), bf16), vmem((BLOCKS, *block), bf16),
            vmem((feat.shape[1] // TILE * W, TILE), f32),
            vmem((feat.shape[1] // TILE, W, TILE), bf16),
            vmem((2 * PAIRS, TILE, CHUNK), bf16), vmem((NONE + 1, *block), bf16), vmem((NONE + 1, *block), bf16),
            vmem(*table), vmem(*table), vmem(*table), pltpu.SMEM(*table), pltpu.SMEM(*table),
            vmem((32, *block), bf16), vmem((32, *block), bf16),
            vmem((64, *block), bf16), vmem((64, *block), bf16),
            vmem((8, *block), bf16), vmem((8, *block), bf16),
            vmem((16, *block), bf16), vmem((16, *block), bf16),
            vmem((2 * LB, *block), bf16),
            vmem((D, CHUNK), bf16), vmem((D, D), bf16), vmem((D, CHUNK), bf16),
            vmem((D, CHUNK), bf16), vmem((D, CHUNK), bf16), vmem((D, CHUNK), bf16),
            vmem((D, D), bf16), vmem((D, CHUNK), bf16), vmem((D, CHUNK), bf16),
            vmem((FEAT, W // 2, D), bf16), vmem((FEAT, W // 2, D), bf16),
            vmem((SIDE, 9, 8, 128), f32), vmem((SIDE, 9, 8, 128), f32),
            vmem((9, 8, 128), f32), vmem((SIDE, 9, 8, 128), f32),
            vmem((9, 8, 128), f32), vmem((SIDE, 9, 8, 128), f32),
            vmem((W // 2, D), f32),
            dma((2 * BATCHES,)), dma((4,)), dma((2,)), dma((2 * BATCHES,)),
            dma, dma((32,)), dma, dma((64,)), dma((2,)), dma((8,)), dma((16,)),
            dma((6,)), dma((2 * FEAT,)), dma((2 * FEAT,)), dma((2 * FEAT,)), dma((2 * FEAT,)), dma((2 * FEAT,)), dma((5,)),
            dma((2,)), dma((16,)), dma((8,)), dma((64,)), dma((32,)), dma((2,)),
            dma((6,)), dma((4,)), dma((FEAT,)), dma((SIDE,)), dma((SIDE,)), dma((SIDE,)), dma,
        ],
        compiler_params=pltpu.CompilerParams(
            collective_id=0, has_side_effects=True, vmem_limit_bytes=VMEM_LIMIT
        ),
    )(doc, label, feat, inc, weight, cot)


def results_kernel(*refs):
    half = len(refs) // 2
    ins, outs, sems = refs[:half], refs[half : 2 * half], refs[-1]
    copies = [pltpu.make_async_copy(i, o, sems.at[k]) for k, (i, o) in enumerate(zip(ins, outs))]
    for copy in copies:
        copy.start()
    for copy in copies:
        copy.wait()


def results(*arrays):
    return pl.pallas_call(
        results_kernel,
        in_specs=[pl.BlockSpec(memory_space=pl.ANY)] * len(arrays),
        out_specs=[pl.BlockSpec(memory_space=pltpu.VMEM)] * len(arrays),
        out_shape=[jax.ShapeDtypeStruct(a.shape, a.dtype) for a in arrays],
        scratch_shapes=[pltpu.SemaphoreType.DMA((len(arrays),))],
    )(*arrays)


def local(features, pair_doc, pair_label, incidence, weight, cotangent):
    act, weight_grad, feature_grad = results(
        *exchange(pair_doc, pair_label, features.T, incidence, weight, cotangent.T)
    )
    return act.T, weight_grad, feature_grad.T


def solution(mesh):
    return jax.shard_map(
        local,
        mesh=mesh,
        in_specs=(
            P("rows", "feat"),
            P("rows"),
            P("rows"),
            P("rows", None, None),
            P("feat", None),
            P("rows", "feat"),
        ),
        out_specs=(P("rows", "feat"), P("feat", None), P("rows", "feat")),
        check_vma=False,
    )
```
